128 devices in a mesh: row: 16 (over y, x), col: 2 (over core), rep: 4 (over z).
Axes of the slice: x: 4, y: 4, z: 4, core: 2. Of those that a mesh axis runs over, the one named last changes fastest.
Arguments:
- amplitudes: bfloat16 [16, 16, 768, 768], P(None, 'rep', ('row', 'col')), may hold values from -6 to 6
- integrals: bfloat16 [16, 768, 16, 768], P('rep', 'row', 'col'), may hold values from -0.0546875 to 0.0546875
- pair_mask: int32 [16, 16], P(None, 'rep'), may hold values 0 or 1
- tile_mask: int32 [16, 6, 16, 6], P('rep', None, 'col'), may hold values 0 or 1
Outputs:
- cycle: float32 [16, 16, 768, 768], P('row', 'col', 'rep')
The draws below stay inside these ranges and needn't reach their ends.
All inputs are finite; a program needn't handle non-finite values. No bound on the sum of `pair_mask` or of `tile_mask` on one device may be relied on, other than what follows from the above.
Results may differ from the reference program's by a relative error of at most 0.0003.
Values may be sent and summed in bfloat16 or wider, within the bound.
A program may use at most 192 MiB of HBM per device.

```python
import jax
import jax.numpy as jnp

O = 16
V = 768
TILE = 128


def touch_ends(values, rng, smallest, high):
    shape = values.shape
    index_at = [jax.random.randint(jax.random.fold_in(rng, axis), (), 0, shape[axis]) for axis in range(len(shape))]
    values = values.at[tuple(index_at)].set(smallest)
    longest = shape.index(max(shape))
    index_at[longest] = (index_at[longest] + 1) % shape[longest]
    return values.at[tuple(index_at)].set(high)


def shard_levels(rng, extent, cuts, least, top_value):
    loudness = 1.0
    for position, blocks in cuts:
        steps = jax.random.uniform(jax.random.fold_in(jax.random.fold_in(rng, 6), position), (blocks,), jnp.float32, least / len(cuts), top_value / len(cuts))
        loudness = loudness * jnp.repeat(jnp.exp(steps), extent[position] // blocks).reshape((-1,) + (1,) * (len(extent) - 1 - position))
    return loudness


def centred(stream_key, dims, scale, limit, cuts=(), kind=jnp.bfloat16):
    gain = shard_levels(stream_key, dims, cuts, -0.22, 0.18) if cuts else 1.0
    result = jax.random.normal(stream_key, dims, jnp.float32) * scale * gain
    return jnp.minimum(jnp.maximum(result, -limit), limit).astype(kind)


def setup_inputs(seed: int = 0) -> dict:
    key_list = jax.random.split(jax.random.key(seed), 5)
    amplitudes = centred(key_list[0], (O, O, V, V), 1.0, 6.0, ((1, 4), (2, 32)))
    integrals = centred(key_list[1], (O, V, O, V), (O * V) ** -0.5, 0.0546875, ((0, 4), (1, 16), (2, 2)))
    pair_mask = touch_ends((jax.random.randint(key_list[2], (O, O), 0, 4) < 3).astype(jnp.int32), jax.random.fold_in(key_list[2], 1), 0, 1)
    tile_mask = touch_ends((jax.random.randint(key_list[3], (O, V // TILE, O, V // TILE), 0, 2) < 1).astype(jnp.int32), jax.random.fold_in(key_list[3], 1), 0, 1)
    return {"amplitudes": amplitudes, "integrals": integrals, "pair_mask": pair_mask, "tile_mask": tile_mask}


def reference(amplitudes, integrals, pair_mask, tile_mask):
    kept = amplitudes * pair_mask[:, :, None, None].astype(amplitudes.dtype)
    spread = jnp.repeat(jnp.repeat(tile_mask, TILE, axis=1), TILE, axis=3)
    sparse = integrals * spread.astype(integrals.dtype)
    left = jnp.transpose(kept, (0, 2, 1, 3)).reshape(O * V, O * V)
    right = sparse.reshape(O * V, O * V)
    product = jnp.dot(left, right, preferred_element_type=jnp.float32)
    return jnp.transpose(product.reshape(O, V, O, V), (0, 2, 1, 3))
```

```python
import jax
import jax.numpy as jnp
from jax import lax
from jax.experimental import pallas as pl
from jax.experimental.pallas import tpu as pltpu
from jax.sharding import PartitionSpec as P

TILE = 128
MESH = pl.DeviceIdType.MESH
NS = 6
NB = 256
QROWS = 192
SROWS = 208
TOP = 32766.0


def quantised(value):
    top = jnp.maximum(jnp.max(jnp.abs(value), axis=0, keepdims=True), 1e-30)
    power = jnp.ceil(jnp.log2(top))
    coded = jnp.round(value * (jnp.exp2(-power) * TOP)).astype(jnp.int16)
    return coded, jnp.broadcast_to(power, (16, NB)).astype(jnp.int16)


def restored(ref):
    power = ref[QROWS:SROWS, :].astype(jnp.float32)[0:1]
    return ref[0:QROWS, :].astype(jnp.float32) * (jnp.exp2(power) * (1.0 / TOP))


def kernel(
    ls, rs, out, lbuf, rbuf, own, tot, zs, zr, xs, xr_,
    la_s, la_r, ld_s, ld_r, lr_s, lr_r, dd_s, dd_r,
    ra_s, ra_r, rd_s, rd_r, rr_s, rr_r, z_s, z_r, x_s, x_r,
):
    row, core, z = lax.axis_index("row"), lax.axis_index("col"), lax.axis_index("rep")
    y, x = row // 4, row % 4

    def at_x(d):
        return (y * 4 + (x + d) % 4, core, z)

    def at_y(d):
        return ((y + d) % 4 * 4 + x, core, z)

    def at_z(d):
        return (row, core, (z + d) % 4)

    partner = (row, 1 - core, z)
    everyone = [f(d) for f in (at_x, at_y, at_z) for d in (1, 2, 3)] + [partner]

    def remote(src, dst, send, recv, device):
        return pltpu.make_async_remote_copy(
            src_ref=src, dst_ref=dst, send_sem=send, recv_sem=recv, device_id=device, device_id_type=MESH
        )

    def arrived(ref, sem):
        pltpu.make_async_copy(ref, ref, sem).wait()

    def off_of(q):
        return jnp.where(q == 0, 2, jnp.where(q == 1, 1, jnp.where(q == 2, 3, 0)))

    def y_of(q):
        return (z + off_of(q)) % 4

    def lpiece(yy, xx, first=0, rows=96, side=None):
        side = core if side is None else side
        return lbuf.at[yy * 4 + xx, pl.ds(pl.multiple_of(side * 96 + first, 16), rows)]

    def la_copy(d):
        return remote(ls.at[(y + d) % 4], lpiece(y, x), la_s.at[d - 1], la_r.at[4 - d], at_y(d))

    def la_local():
        return pltpu.make_async_copy(ls.at[y], lpiece(y, x), la_r.at[0])

    def ld_copy(q, way):
        ref = lpiece(y_of(q), x)
        return remote(ref, ref, ld_s.at[q, way], ld_r.at[q, way], at_x(1 if way == 0 else 3))

    def lr_copy(q, way):
        ref = lpiece(y_of(q), (x + (3 if way == 0 else 1)) % 4, 48 * way, 48)
        return remote(ref, ref, lr_s.at[q, way], lr_r.at[q, way], at_x(1 if way == 0 else 3))

    def dd_copy(q, xr):
        ref = lpiece(y_of(q), (x + xr) % 4)
        return remote(ref, ref, dd_s.at[q, xr], dd_r.at[q, xr], partner)

    def rpiece(s, xx):
        return rbuf.at[s, :, pl.ds(pl.multiple_of((y * 4 + xx) * 48, 16), 48), :]

    def rblock(s, yy, k0=0, nk=4):
        return rbuf.at[s, pl.ds(k0, nk), pl.ds(pl.multiple_of(yy * 192, 16), 192), :]

    def ra_copy(s, d):
        return remote(rs.at[(x + d) % 4, s], rpiece(s, x), ra_s.at[s, d - 1], ra_r.at[s, 4 - d], at_x(d))

    def ra_local(s):
        return pltpu.make_async_copy(rs.at[x, s], rpiece(s, x), ra_r.at[s, 0])

    def rd_copy(s, way):
        ref = rblock(s, y)
        return remote(ref, ref, rd_s.at[s, way], rd_r.at[s, way], at_y(1 if way == 0 else 3))

    def rr_copy(s, way):
        ref = rblock(s, (y + (3 if way == 0 else 1)) % 4, 2 * way, 2)
        return remote(ref, ref, rr_s.at[s, way], rr_r.at[s, way], at_y(1 if way == 0 else 3))

    def z_copy(q, xr, s):
        return remote(zs.at[q, xr, s], zr.at[q, xr, s], z_s.at[q, xr, s], z_r.at[q, xr, s], at_z(off_of(q)))

    def x_copy(s, d):
        return remote(xs.at[s, d - 1], xr_.at[s, d - 1], x_s.at[s, d - 1], x_r.at[s, d - 1], at_x(d))

    def ra_start(s):
        for d in (1, 3, 2):
            ra_copy(s, d).start()

    def rd_start(s):
        for d in range(4):
            arrived(rpiece(s, (x + d) % 4), ra_r.at[s, d])
        for way in (0, 1):
            rd_copy(s, way).start()

    def rr_start(s):
        for way in (0, 1):
            arrived(rblock(s, (y + (3 if way == 0 else 1)) % 4), rd_r.at[s, way])
            rr_copy(s, way).start()

    def rr_wait(s):
        for way in (0, 1):
            arrived(rblock(s, (y + 2) % 4, 2 * way, 2), rr_r.at[s, way])

    def ld_start(q):
        for way in (0, 1):
            ld_copy(q, way).start()

    def lr_start(q):
        for way in (0, 1):
            xr = 3 if way == 0 else 1
            arrived(lpiece(y_of(q), (x + xr) % 4), ld_r.at[q, way])
            lr_copy(q, way).start()
            dd_copy(q, xr).start()

    def lr_done(q):
        for way in (0, 1):
            arrived(lpiece(y_of(q), (x + 2) % 4, 48 * way, 48), lr_r.at[q, way])
        dd_copy(q, 2).start()

    def dd_wait(q, xr):
        arrived(lpiece(y_of(q), (x + xr) % 4, side=1 - core), dd_r.at[q, xr])

    def product(q, xr, s):
        src = y_of(q) * 4 + (x + xr) % 4
        value = jnp.dot(lbuf[src], rbuf[s].reshape(3072, NB), preferred_element_type=jnp.float32)

        @pl.when(q == 3)
        def _():
            own[s, xr] = value

        @pl.when(q < 3)
        def _():
            coded, power = quantised(value)
            zs[q, xr, s, 0:QROWS, :] = coded
            zs[q, xr, s, QROWS:SROWS, :] = power
            z_copy(q, xr, s).start()

    barrier = pltpu.get_barrier_semaphore()
    for device in everyone:
        pl.semaphore_signal(barrier, inc=1, device_id=device, device_id_type=MESH)
    pl.semaphore_wait(barrier, len(everyone))

    ra_start(0)
    for d in (1, 3, 2):
        la_copy(d).start()
    la_local().start()
    for s in range(NS):
        ra_local(s).start()
    ra_start(1)
    ra_start(2)
    rd_start(0)
    rd_start(1)

    def own_column(q, carry):
        yy = y_of(q)
        arrived(lpiece(yy, x), la_r.at[(yy - y + 4) % 4])

        @pl.when(q < 2)
        def _():
            ld_start(q)

        dd_copy(q, 0).start()
        return carry

    lax.fori_loop(0, 4, own_column, 0)
    rr_start(0)

    def step(s, carry):
        @pl.when(s < NS - 3)
        def _():
            ra_start(s + 3)

        @pl.when(s < NS - 2)
        def _():
            rd_start(s + 2)

        @pl.when(s < NS - 1)
        def _():
            rr_start(s + 1)

        @pl.when(s < 4)
        def _():
            lr_start(s)

        @pl.when((s >= 1) & (s < 3))
        def _():
            ld_start(s + 1)

        @pl.when((s >= 1) & (s < 5))
        def _():
            lr_done(s - 1)

        rr_wait(s)

        @pl.when(s == 0)
        def _():
            for q in range(4):
                dd_wait(q, 0)

        before = 4 + 3 * jnp.maximum(s - 1, 0)
        fresh = jnp.where((s >= 1) & (s < 5), 3 * (s + 1), 0)

        def one(n, carry):
            m = n - before
            late = n >= before
            first = n < 4
            q = jnp.where(late, s - 1, jnp.where(first, n, (n - 4) // 3))
            xr = jnp.where(late, 1 + m % 3, jnp.where(first, 0, 1 + (n - 4) % 3))
            part = jnp.where(late, m // 3, s)

            @pl.when(late & (m < 3))
            def _():
                dd_wait(q, xr)

            product(q, xr, part)
            return carry

        lax.fori_loop(0, before + fresh, one, 0)
        return carry

    lax.fori_loop(0, NS, step, 0)

    def reduce(s):
        jj, bt = s // 3, s % 3

        def gather(xr, carry):
            total = own[s, xr]
            for q in range(3):
                arrived(zr.at[q, xr, s], z_r.at[q, xr, s])
                total = total + restored(zr.at[q, xr, s])
            tot[(x + xr) % 4] = total
            return carry

        lax.fori_loop(0, 4, gather, 0)

        def rows_of(i):
            return jnp.concatenate(
                [
                    tot[xx, pl.ds(pl.multiple_of(side * 96 + i * 24, 8), 24), :]
                    for xx in range(4)
                    for side in range(2)
                ],
                axis=0,
            )

        def give(d, carry):
            coded, power = quantised(rows_of((x + d) % 4))
            xs[s, d - 1, 0:QROWS, :] = coded
            xs[s, d - 1, QROWS:SROWS, :] = power
            x_copy(s, d).start()
            return carry

        lax.fori_loop(1, 4, give, 0)
        out[0, x * 2 + jj, :, pl.ds(pl.multiple_of(bt * NB, NB), NB)] = rows_of(x)

    def finish(s):
        jj, bt = s // 3, s % 3

        def take(d, carry):
            arrived(xr_.at[s, d - 1], x_r.at[s, d - 1])
            xx = (x - d + 4) % 4
            out[0, xx * 2 + jj, :, pl.ds(pl.multiple_of(bt * NB, NB), NB)] = restored(xr_.at[s, d - 1])
            return carry

        lax.fori_loop(1, 4, take, 0)

    def tail(s, carry):
        @pl.when(s < NS)
        def _():
            reduce(s)

        @pl.when(s >= 1)
        def _():
            finish(s - 1)

        return carry

    lax.fori_loop(0, NS + 1, tail, 0)

    for d in (1, 2, 3):
        la_copy(d).wait_send()

    def sent_right(s, carry):
        for d in (1, 2, 3):
            ra_copy(s, d).wait_send()
            x_copy(s, d).wait_send()
        for way in (0, 1):
            rd_copy(s, way).wait_send()
            rr_copy(s, way).wait_send()
        return carry

    def sent_left(q, carry):
        for way in (0, 1):
            ld_copy(q, way).wait_send()
            lr_copy(q, way).wait_send()
        for xr in range(4):
            dd_copy(q, xr).wait_send()
        return carry

    def sent_z(n, carry):
        z_copy(n // 24, n // 6 % 4, n % 6).wait_send()
        return carry

    lax.fori_loop(0, NS, sent_right, 0)
    lax.fori_loop(0, 4, sent_left, 0)
    lax.fori_loop(0, 72, sent_z, 0)


def on_device(amplitudes, integrals, pair_mask, tile_mask):
    kept = amplitudes * pair_mask[:, :, None, None].astype(jnp.bfloat16)
    ls = kept.transpose(0, 2, 1, 3).reshape(4, 96, 3072)
    krows, cwidth, jcols, bwidth = integrals.shape
    ntiles = tile_mask.shape[1]
    cglobal = lax.axis_index("row") * cwidth + jnp.arange(cwidth, dtype=jnp.int32)
    onehot = (cglobal[:, None] // TILE == jnp.arange(ntiles, dtype=jnp.int32)[None, :]).astype(jnp.float32)
    rowmask = jnp.einsum("ktjs,ct->kcjs", tile_mask.astype(jnp.float32), onehot)
    fullmask = jnp.repeat(rowmask, TILE, axis=3)
    sparse = integrals * fullmask.astype(jnp.bfloat16)
    rs = sparse.reshape(krows, cwidth, 4, 2, 3, NB).transpose(2, 3, 4, 0, 1, 5).reshape(4, NS, krows, cwidth, NB)
    dma = pltpu.SemaphoreType.DMA
    bf, i16, f32 = jnp.bfloat16, jnp.int16, jnp.float32
    return pl.pallas_call(
        kernel,
        out_shape=jax.ShapeDtypeStruct((1, 8, QROWS, 768), f32),
        in_specs=[pl.BlockSpec(memory_space=pl.ANY)] * 2,
        out_specs=pl.BlockSpec(memory_space=pltpu.VMEM),
        scratch_shapes=[
            pltpu.VMEM((16, 192, 3072), bf),
            pltpu.VMEM((NS, 4, 768, NB), bf),
            pltpu.VMEM((NS, 4, QROWS, NB), f32),
            pltpu.VMEM((4, QROWS, NB), f32),
            pltpu.VMEM((3, 4, NS, SROWS, NB), i16),
            pltpu.VMEM((3, 4, NS, SROWS, NB), i16),
            pltpu.VMEM((NS, 3, SROWS, NB), i16),
            pltpu.VMEM((NS, 3, SROWS, NB), i16),
            dma((3,)), dma((4,)), dma((4, 2)), dma((4, 2)), dma((4, 2)), dma((4, 2)), dma((4, 4)), dma((4, 4)),
            dma((NS, 3)), dma((NS, 4)), dma((NS, 2)), dma((NS, 2)), dma((NS, 2)), dma((NS, 2)),
            dma((3, 4, NS)), dma((3, 4, NS)), dma((NS, 3)), dma((NS, 3)),
        ],
        compiler_params=pltpu.CompilerParams(
            collective_id=0, has_side_effects=True, vmem_limit_bytes=63 * 2**20
        ),
        cost_estimate=pl.CostEstimate(flops=29 * 10**9, bytes_accessed=10**7, transcendentals=0),
    )(ls, rs)


def solution(mesh):
    placed = (
        P(None, "rep", ("row", "col"), None),
        P("rep", "row", "col", None),
        P(None, "rep"),
        P("rep", None, "col", None),
    )
    return jax.shard_map(
        on_device,
        mesh=mesh,
        in_specs=placed,
        out_specs=P("row", "col", "rep", None),
        check_vma=False,
    )
```

```python
import jax
import jax.numpy as jnp
from jax import lax
from jax.experimental import pallas as pl
from jax.experimental.pallas import tpu as pltpu
from jax.sharding import PartitionSpec as P

TILE = 128
MESH = pl.DeviceIdType.MESH
NS = 6
NB = 256
QROWS = 192
SROWS = 208
HROWS = 96
HS = 112
PARTS = ((0, 1, 3), (2,))
TOP = 32766.0


EVENTS = (
    (0, "ra", 0), (0, "ra", 1), (0, "ra", 2), (0, "LA", 0), (0, "ld", 0), (0, "ra", 3), (0, "la", 1),
    (0, "la", 3), (0, "RA", 0), (0, "rd", 0), (0, "la", 2), (0, "RA", 1), (0, "LA", 1), (0, "LA", 2),
    (0, "ld", 2), (0, "ld", 1), (0, "RD", 0), (0, "LD", 0), (0, "rr", 0), (0, "rd", 1), (0, "RA", 2),
    (0, "rd", 2), (0, "RA", 3), (0, "LA", 3), (0, "ld", 3), (0, "ra", 4), (0, "RR", 0), (0, "DD", (0, 0)),
    (1, "DD", (1, 0)), (2, "DD", (2, 0)), (3, "DD", (3, 0)), (4, "DD", (0, 1)), (5, "LD", 2), (5, "lr", 2),
    (5, "ra", 5), (5, "lr", 0), (5, "RD", 1), (5, "rr", 1), (5, "DD", (2, 1)), (6, "RD", 2), (6, "LD", 1),
    (6, "rr", 2), (6, "rd", 3), (6, "RR", 1), (10, "DD", (1, 1)), (12, "RR", 2), (18, "LD", 3), (18, "lr", 3),
    (18, "lr", 1), (21, "RA", 4), (21, "RD", 3), (21, "rr", 3), (21, "rd", 4), (21, "DD", (3, 1)),
    (24, "RR", 3), (25, "LR", 2), (31, "RA", 5), (31, "rd", 5), (32, "DD", (2, 2)), (36, "RD", 4),
    (36, "rr", 4), (36, "LR", 0), (36, "DD", (0, 2)), (40, "RD", 5), (40, "rr", 5), (40, "LR", 3),
    (40, "DD", (3, 2)), (42, "RR", 4), (47, "LR", 1), (48, "RR", 5), (58, "DD", (1, 2)),
)
BLOCKS = (
    (0, 0, 0), (1, 0, 0), (2, 0, 0), (3, 0, 0), (0, 1, 0), (2, 1, 0), (0, 0, 1), (1, 0, 1), (2, 0, 1),
    (3, 0, 1), (1, 1, 0), (0, 1, 1), (0, 0, 2), (1, 0, 2), (2, 0, 2), (3, 0, 2), (1, 1, 1), (2, 1, 1),
    (0, 1, 2), (1, 1, 2), (2, 1, 2), (3, 1, 0), (3, 1, 1), (3, 1, 2), (0, 0, 3), (1, 0, 3), (2, 0, 3),
    (3, 0, 3), (0, 1, 3), (1, 1, 3), (2, 1, 3), (3, 1, 3), (2, 2, 0), (2, 2, 1), (2, 2, 2), (2, 2, 3),
    (0, 2, 0), (0, 2, 1), (0, 2, 2), (0, 2, 3), (3, 2, 0), (3, 2, 1), (0, 0, 4), (1, 0, 4), (2, 0, 4),
    (3, 0, 4), (0, 1, 4), (1, 1, 4), (0, 0, 5), (1, 0, 5), (2, 0, 5), (3, 0, 5), (2, 1, 4), (3, 1, 4),
    (0, 1, 5), (1, 1, 5), (2, 1, 5), (3, 1, 5), (1, 2, 0), (1, 2, 1), (1, 2, 2), (3, 2, 2), (1, 2, 3),
    (3, 2, 3), (0, 2, 4), (1, 2, 4), (2, 2, 4), (3, 2, 4), (0, 2, 5), (1, 2, 5), (2, 2, 5), (3, 2, 5),
)
LAG = 10
SUMS = ((47, 47, 47, 49, 71, 75), (76, 77, 79, 81, 81, 81))
ROUNDS = 82


def quantised(value):
    top = jnp.maximum(jnp.max(jnp.abs(value), axis=0, keepdims=True), 1e-30)
    power = jnp.ceil(jnp.log2(top))
    coded = jnp.round(value * (jnp.exp2(-power) * TOP)).astype(jnp.int16)
    return coded, jnp.broadcast_to(power, (16, NB)).astype(jnp.int16)


def restored(ref, rows=QROWS):
    power = ref[rows : rows + 16, :].astype(jnp.float32)[0:1]
    return ref[0:rows, :].astype(jnp.float32) * (jnp.exp2(power) * (1.0 / TOP))


def kernel(
    ls, rs, out, lbuf, rbuf, own, tot, val, hs, hr, zs, zr, xs0, xr0, xs1, xr1,
    la_s, la_r, ld_s, ld_r, lr_s, lr_r, dd_s, dd_r,
    ra_s, ra_r, rd_s, rd_r, rr_s, rr_r, h_s, h_r, z_s, z_r, x0_s, x0_r, x1_s, x1_r,
):
    row, core, z = lax.axis_index("row"), lax.axis_index("col"), lax.axis_index("rep")
    y, x = row // 4, row % 4

    def at_x(d):
        return (y * 4 + (x + d) % 4, core, z)

    def at_y(d):
        return ((y + d) % 4 * 4 + x, core, z)

    def at_z(d):
        return (row, core, (z + d) % 4)

    partner = (row, 1 - core, z)
    everyone = [f(d) for f in (at_x, at_y, at_z) for d in (1, 2, 3)] + [partner]

    def remote(src, dst, send, recv, device):
        return pltpu.make_async_remote_copy(
            src_ref=src, dst_ref=dst, send_sem=send, recv_sem=recv, device_id=device, device_id_type=MESH
        )

    def arrived(ref, sem):
        pltpu.make_async_copy(ref, ref, sem).wait()

    def rel_of(p):
        return jnp.where(p < 2, p, 5 - p)

    def y_at(p):
        return (y + rel_of(p)) % 4

    def lpiece(yy, xx, first=0, rows=96, side=None):
        side = core if side is None else side
        return lbuf.at[yy * 4 + xx, :, pl.ds(pl.multiple_of(side * 96 + first, 16), rows), :]

    def la_copy(d):
        return remote(ls.at[(y + d) % 4], lpiece(y, x), la_s.at[d - 1], la_r.at[4 - d], at_y(d))

    def la_local():
        return pltpu.make_async_copy(ls.at[y], lpiece(y, x), la_r.at[0])

    def ld_copy(p, way):
        ref = lpiece(y_at(p), x)
        return remote(ref, ref, ld_s.at[p, way], ld_r.at[p, way], at_x(1 if way == 0 else 3))

    def lr_copy(p, way):
        ref = lpiece(y_at(p), (x + (3 if way == 0 else 1)) % 4, 48 * way, 48)
        return remote(ref, ref, lr_s.at[p, way], lr_r.at[p, way], at_x(1 if way == 0 else 3))

    def dd_copy(p, xr):
        ref = lpiece(y_at(p), (x + xr) % 4)
        return remote(ref, ref, dd_s.at[p, xr], dd_r.at[p, xr], partner)

    def rpiece(s, xx):
        return rbuf.at[s, :, pl.ds(pl.multiple_of((y * 4 + xx) * 48, 16), 48), :]

    def rblock(s, yy, k0=0, nk=4):
        return rbuf.at[s, pl.ds(k0, nk), pl.ds(pl.multiple_of(yy * 192, 16), 192), :]

    def ra_copy(s, d):
        return remote(rs.at[(x + d) % 4, s], rpiece(s, x), ra_s.at[s, d - 1], ra_r.at[s, 4 - d], at_x(d))

    def ra_local(s):
        return pltpu.make_async_copy(rs.at[x, s], rpiece(s, x), ra_r.at[s, 0])

    def rd_copy(s, way):
        ref = rblock(s, y)
        return remote(ref, ref, rd_s.at[s, way], rd_r.at[s, way], at_y(1 if way == 0 else 3))

    def rr_copy(s, way):
        ref = rblock(s, (y + (3 if way == 0 else 1)) % 4, 2 * way, 2)
        return remote(ref, ref, rr_s.at[s, way], rr_r.at[s, way], at_y(1 if way == 0 else 3))

    def h_copy(xr, s, way):
        return remote(
            hs.at[xr, s, way], hr.at[xr, s, way], h_s.at[xr, s, way], h_r.at[xr, s, way], at_z(1 if way == 0 else 3)
        )

    def z_copy(way, xr, s):
        return remote(
            zs.at[way, xr, s], zr.at[way, xr, s], z_s.at[way, xr, s], z_r.at[way, xr, s], at_z(1 + 2 * way)
        )

    def x0_copy(s, d):
        return remote(xs0.at[s, d - 1], xr0.at[s, d - 1], x0_s.at[s, d - 1], x0_r.at[s, d - 1], at_x(d))

    def x1_copy(s, d):
        return remote(xs1.at[s, d - 1], xr1.at[s, d - 1], x1_s.at[s, d - 1], x1_r.at[s, d - 1], at_x(d))

    def ra_start(s):
        for d in (1, 3, 2):
            ra_copy(s, d).start()

    def ra_wait(s):
        for d in range(4):
            arrived(rpiece(s, (x + d) % 4), ra_r.at[s, d])

    def rd_start(s):
        for way in (0, 1):
            rd_copy(s, way).start()

    def rd_wait(s):
        for way in (0, 1):
            arrived(rblock(s, (y + (3 if way == 0 else 1)) % 4), rd_r.at[s, way])

    def rr_start(s):
        for way in (0, 1):
            rr_copy(s, way).start()

    def rr_wait(s):
        for way in (0, 1):
            arrived(rblock(s, (y + 2) % 4, 2 * way, 2), rr_r.at[s, way])

    def la_wait(p):
        d = rel_of(p)
        arrived(lpiece(y_at(p), x), la_r.at[d])
        dd_copy(p, 0).start()

    def ld_start(p):
        for way in (0, 1):
            ld_copy(p, way).start()

    def ld_wait(p):
        for way in (0, 1):
            xr = 3 if way == 0 else 1
            arrived(lpiece(y_at(p), (x + xr) % 4), ld_r.at[p, way])
            dd_copy(p, xr).start()

    def lr_start(p):
        for way in (0, 1):
            lr_copy(p, way).start()

    def lr_done(p):
        for way in (0, 1):
            arrived(lpiece(y_at(p), (x + 2) % 4, 48 * way, 48), lr_r.at[p, way])
        dd_copy(p, 2).start()

    def dd_wait(p, xr):
        arrived(lpiece(y_at(p), (x + xr) % 4, side=1 - core), dd_r.at[p, xr])

    def product(p, pieces, s):
        left = jnp.concatenate(
            [
                jnp.concatenate([lbuf[y_at(p) * 4 + (x + xr) % 4, k] for k in range(4)], axis=1)
                for xr in pieces
            ],
            axis=0,
        )
        return jnp.dot(left, rbuf[s].reshape(3072, NB), preferred_element_type=jnp.float32)

    def give_on(value, off, xr, s):
        @pl.when(off == 0)
        def _():
            own[s, xr] = value

        @pl.when(off == 2)
        def _():
            for way in (0, 1):
                coded, power = quantised(value[HROWS * way : HROWS * (way + 1)])
                hs[xr, s, way, 0:HROWS, :] = coded
                hs[xr, s, way, HROWS:HS, :] = power
                h_copy(xr, s, way).start()

        for way in (0, 1):

            @pl.when(off == 1 + 2 * way)
            def _(way=way):
                arrived(hr.at[xr, s, way], h_r.at[xr, s, way])
                more = restored(hr.at[xr, s, way], HROWS)
                first, second = value[0:HROWS], value[HROWS:QROWS]
                if way == 0:
                    first = first + more
                else:
                    second = second + more
                coded, power = quantised(jnp.concatenate([first, second], axis=0))
                zs[way, xr, s, 0:QROWS, :] = coded
                zs[way, xr, s, QROWS:SROWS, :] = power
                z_copy(way, xr, s).start()

    barrier = pltpu.get_barrier_semaphore()
    for device in everyone:
        pl.semaphore_signal(barrier, inc=1, device_id=device, device_id_type=MESH)
    pl.semaphore_wait(barrier, len(everyone))

    la_local().start()
    for s in range(NS):
        ra_local(s).start()

    does = {
        "ra": ra_start, "rd": rd_start, "rr": rr_start, "ld": ld_start, "lr": lr_start,
        "la": lambda d: la_copy(d).start(),
        "RA": ra_wait, "RD": rd_wait, "RR": rr_wait, "LA": la_wait, "LD": ld_wait, "LR": lr_done,
        "DD": lambda k: [dd_wait(k[0], xr) for xr in ((0,), (1, 3), (2,))[k[1]]],
    }

    def look(i):
        codes = [p * 32 + kind * 8 + s for p, kind, s in BLOCKS]
        word = 0
        for n in range(0, len(codes), 4):
            word = jnp.where(i // 4 == n // 4, sum(c * 128**m for m, c in enumerate(codes[n : n + 4])), word)
        m = i % 4
        shift = jnp.where(m == 0, 1, jnp.where(m == 1, 128, jnp.where(m == 2, 128**2, 128**3)))
        code = word // shift % 128
        return (i >= 0) & (i < len(codes)), code // 32, code // 8 % 4, code % 8

    def reduce(s, part):
        jj, bt = s // 3, s % 3
        pieces = PARTS[part]
        rows = 48 * len(pieces)
        sent, begin = (xs0, x0_copy) if part == 0 else (xs1, x1_copy)
        for xr in pieces:
            total = own[s, xr]
            for way in (0, 1):
                arrived(zr.at[way, xr, s], z_r.at[way, xr, s])
                total = total + restored(zr.at[way, xr, s])
            tot[xr] = total

        def rows_of(i):
            return [
                tot[xr, pl.ds(pl.multiple_of(side * 96 + i * 24, 8), 24), :] for xr in pieces for side in range(2)
            ]

        def give(d, carry):
            coded, power = quantised(jnp.concatenate(rows_of((x + d) % 4), axis=0))
            sent[s, d - 1, 0:rows, :] = coded
            sent[s, d - 1, rows : rows + 16, :] = power
            begin(s, d).start()
            return carry

        lax.fori_loop(1, 4, give, 0)
        place(s, part, x, jnp.concatenate(rows_of(x), axis=0))

    def place(s, part, source, value):
        jj, bt = s // 3, s % 3
        for n, xr in enumerate(PARTS[part]):
            at = pl.multiple_of((source + xr) % 4 * 48, 8)
            out[0, source * 2 + jj, pl.ds(at, 48), pl.ds(pl.multiple_of(bt * NB, NB), NB)] = value[48 * n : 48 * n + 48]

    def round_(i, carry):
        for n in range(len(BLOCKS) + 1):
            todo = [(what, k) for m, what, k in EVENTS if m == n]
            if todo:

                @pl.when(i == n)
                def _(todo=todo):
                    for what, k in todo:
                        does[what](k)

        def half(j, carry):
            there, p, kind, s = look(i - LAG * j)
            off = (y_at(p) - z + 4) % 4

            @pl.when(there & (off % 2 == j))
            def _():
                @pl.when(kind == 1)
                def _():
                    val[...] = product(p, (1, 3), s).reshape(2, QROWS, NB)

                @pl.when(kind != 1)
                def _():
                    val[0] = product(p, (kind,), s)

                def one(n, carry):
                    give_on(val[n], off, jnp.where(kind == 1, 1 + 2 * n, kind), s)
                    return carry

                lax.fori_loop(0, jnp.where(kind == 1, 2, 1), one, 0)

            return carry

        lax.fori_loop(0, 2, half, 0)

        for part in range(2):

            def sums(s, carry, part=part):
                reduce(s, part)
                return carry

            begun = sum(jnp.where(i > n, 1, 0) for n in SUMS[part])
            lax.fori_loop(begun, sum(jnp.where(i >= n, 1, 0) for n in SUMS[part]), sums, 0)
        return carry

    lax.fori_loop(0, ROUNDS, round_, 0)

    def finish(s, carry):
        def take(d, carry):
            arrived(xr0.at[s, d - 1], x0_r.at[s, d - 1])
            place(s, 0, (x - d + 4) % 4, restored(xr0.at[s, d - 1], 144))
            arrived(xr1.at[s, d - 1], x1_r.at[s, d - 1])
            place(s, 1, (x - d + 4) % 4, restored(xr1.at[s, d - 1], 48))
            return carry

        return lax.fori_loop(1, 4, take, carry)

    lax.fori_loop(0, NS, finish, 0)

    for d in (1, 2, 3):
        la_copy(d).wait_send()

    def sent_right(s, carry):
        for d in (1, 2, 3):
            ra_copy(s, d).wait_send()
            x0_copy(s, d).wait_send()
            x1_copy(s, d).wait_send()
        for way in (0, 1):
            rd_copy(s, way).wait_send()
            rr_copy(s, way).wait_send()
        return carry

    def sent_left(q, carry):
        for way in (0, 1):
            ld_copy(q, way).wait_send()
            lr_copy(q, way).wait_send()
        for xr in range(4):
            dd_copy(q, xr).wait_send()
        return carry

    def sent_z(n, carry):
        for way in (0, 1):
            h_copy(n // 6, n % 6, way).wait_send()
            z_copy(way, n // 6, n % 6).wait_send()
        return carry

    lax.fori_loop(0, NS, sent_right, 0)
    lax.fori_loop(0, 4, sent_left, 0)
    lax.fori_loop(0, 24, sent_z, 0)


def right_kernel(mask, w, rs):
    k = pl.program_id(0)
    first = lax.axis_index("row") * 48
    tile = first // TILE
    after = jnp.minimum(tile + 1, 5)
    edge = (tile + 1) * TILE - first
    upper = lax.broadcasted_iota(jnp.int32, (48, TILE), 0) < edge
    rows = jnp.swapaxes(w[0].astype(jnp.float32), 0, 1)
    for j in range(8):
        for b in range(6):
            kept = jnp.where(upper, mask[k, tile, j, b].astype(jnp.float32), mask[k, after, j, b].astype(jnp.float32))
            rs[j // 2, j % 2 * 3 + b // 2, 0, :, b % 2 * TILE : (b % 2 + 1) * TILE] = (
                rows[j, :, b * TILE : (b + 1) * TILE] * kept
            ).astype(jnp.bfloat16)


def on_device(amplitudes, integrals, pair_mask, tile_mask):
    kept = amplitudes * pair_mask[:, :, None, None].astype(jnp.bfloat16)
    ls = kept.reshape(4, 4, 4, 24, 768).transpose(0, 2, 1, 3, 4).reshape(4, 4, 96, 768)
    rs = pl.pallas_call(
        right_kernel,
        grid=(4,),
        out_shape=jax.ShapeDtypeStruct((4, NS, 4, 48, NB), jnp.bfloat16),
        in_specs=[
            pl.BlockSpec(memory_space=pltpu.SMEM),
            pl.BlockSpec((1, 48, 8, 768), lambda k: (k, 0, 0, 0)),
        ],
        out_specs=pl.BlockSpec((4, NS, 1, 48, NB), lambda k: (0, 0, k, 0, 0)),
        cost_estimate=pl.CostEstimate(flops=10**6, bytes_accessed=5 * 10**6, transcendentals=0),
    )(tile_mask, integrals)
    dma = pltpu.SemaphoreType.DMA
    bf, i16, f32 = jnp.bfloat16, jnp.int16, jnp.float32
    return pl.pallas_call(
        kernel,
        out_shape=jax.ShapeDtypeStruct((1, 8, QROWS, 768), f32),
        in_specs=[pl.BlockSpec(memory_space=pl.ANY)] * 2,
        out_specs=pl.BlockSpec(memory_space=pltpu.VMEM),
        scratch_shapes=[
            pltpu.VMEM((16, 4, 192, 768), bf),
            pltpu.VMEM((NS, 4, 768, NB), bf),
            pltpu.VMEM((NS, 4, QROWS, NB), f32),
            pltpu.VMEM((4, QROWS, NB), f32),
            pltpu.VMEM((2, QROWS, NB), f32),
            pltpu.VMEM((4, NS, 2, HS, NB), i16),
            pltpu.VMEM((4, NS, 2, HS, NB), i16),
            pltpu.VMEM((2, 4, NS, SROWS, NB), i16),
            pltpu.VMEM((2, 4, NS, SROWS, NB), i16),
            pltpu.VMEM((NS, 3, 160, NB), i16),
            pltpu.VMEM((NS, 3, 160, NB), i16),
            pltpu.VMEM((NS, 3, 64, NB), i16),
            pltpu.VMEM((NS, 3, 64, NB), i16),
            dma((3,)), dma((4,)), dma((4, 2)), dma((4, 2)), dma((4, 2)), dma((4, 2)), dma((4, 4)), dma((4, 4)),
            dma((NS, 3)), dma((NS, 4)), dma((NS, 2)), dma((NS, 2)), dma((NS, 2)), dma((NS, 2)),
            dma((4, NS, 2)), dma((4, NS, 2)), dma((2, 4, NS)), dma((2, 4, NS)), dma((NS, 3)), dma((NS, 3)),
            dma((NS, 3)), dma((NS, 3)),
        ],
        compiler_params=pltpu.CompilerParams(
            collective_id=0, has_side_effects=True, vmem_limit_bytes=63 * 2**20
        ),
        cost_estimate=pl.CostEstimate(flops=29 * 10**9, bytes_accessed=10**7, transcendentals=0),
    )(ls, rs)


def solution(mesh):
    placed = (
        P(None, "rep", ("row", "col"), None),
        P("rep", "row", "col", None),
        P(None, "rep"),
        P("rep", None, "col", None),
    )
    return jax.shard_map(
        on_device,
        mesh=mesh,
        in_specs=placed,
        out_specs=P("row", "col", "rep", None),
        check_vma=False,
    )
```

```python
import jax
import jax.numpy as jnp
from jax import lax
from jax.experimental import pallas as pl
from jax.experimental.pallas import tpu as pltpu
from jax.sharding import PartitionSpec as P

TILE = 128
MESH = pl.DeviceIdType.MESH
NS = 6
NB = 256
QROWS = 192
HROWS = 96


def coded_shape(rows):
    return (2 * rows + 16, 128)


PARTS = ((0, 1, 3), (2,))
TOP = 32766.0


EVENTS = (
    (0, "ra", 0), (0, "ra", 1), (0, "ra", 2), (0, "LA", 0), (0, "ld", 0), (0, "ra", 3), (0, "la", 1),
    (0, "la", 3), (0, "RA", 0), (0, "rd", 0), (0, "la", 2), (0, "RA", 1), (0, "LA", 1), (0, "LA", 2),
    (0, "ld", 2), (0, "ld", 1), (0, "RD", 0), (0, "LD", 0), (0, "rr", 0), (0, "rd", 1), (0, "RA", 2),
    (0, "rd", 2), (0, "RA", 3), (0, "LA", 3), (0, "ld", 3), (0, "ra", 4), (0, "RR", 0), (0, "DD", (0, 0)),
    (1, "DD", (1, 0)), (2, "DD", (2, 0)), (3, "DD", (3, 0)), (4, "DD", (0, 1)), (5, "LD", 2), (5, "lr", 2),
    (5, "ra", 5), (5, "lr", 0), (5, "RD", 1), (5, "rr", 1), (5, "DD", (2, 1)), (6, "RD", 2), (6, "LD", 1),
    (6, "rr", 2), (6, "rd", 3), (6, "RR", 1), (10, "DD", (1, 1)), (12, "RR", 2), (18, "LD", 3), (18, "lr", 3),
    (18, "lr", 1), (21, "RA", 4), (21, "RD", 3), (21, "rr", 3), (21, "rd", 4), (21, "DD", (3, 1)),
    (24, "RR", 3), (25, "LR", 2), (31, "RA", 5), (31, "rd", 5), (32, "DD", (2, 2)), (36, "RD", 4),
    (36, "rr", 4), (36, "LR", 0), (36, "DD", (0, 2)), (40, "RD", 5), (40, "rr", 5), (40, "LR", 3),
    (40, "DD", (3, 2)), (42, "RR", 4), (47, "LR", 1), (48, "RR", 5), (58, "DD", (1, 2)),
)
BLOCKS = (
    (0, 0, 0), (1, 0, 0), (2, 0, 0), (3, 0, 0), (0, 1, 0), (2, 1, 0), (0, 0, 1), (1, 0, 1), (2, 0, 1),
    (3, 0, 1), (1, 1, 0), (0, 1, 1), (0, 0, 2), (1, 0, 2), (2, 0, 2), (3, 0, 2), (1, 1, 1), (2, 1, 1),
    (0, 1, 2), (1, 1, 2), (2, 1, 2), (3, 1, 0), (3, 1, 1), (3, 1, 2), (0, 0, 3), (1, 0, 3), (2, 0, 3),
    (3, 0, 3), (0, 1, 3), (1, 1, 3), (2, 1, 3), (3, 1, 3), (2, 2, 0), (2, 2, 1), (2, 2, 2), (2, 2, 3),
    (0, 2, 0), (0, 2, 1), (0, 2, 2), (0, 2, 3), (3, 2, 0), (3, 2, 1), (0, 0, 4), (1, 0, 4), (2, 0, 4),
    (3, 0, 4), (0, 1, 4), (1, 1, 4), (0, 0, 5), (1, 0, 5), (2, 0, 5), (3, 0, 5), (2, 1, 4), (3, 1, 4),
    (0, 1, 5), (1, 1, 5), (2, 1, 5), (3, 1, 5), (1, 2, 0), (1, 2, 1), (1, 2, 2), (3, 2, 2), (1, 2, 3),
    (3, 2, 3), (0, 2, 4), (1, 2, 4), (2, 2, 4), (3, 2, 4), (0, 2, 5), (1, 2, 5), (2, 2, 5), (3, 2, 5),
)
LAG = 10
SUMS = ((47, 47, 47, 49, 71, 75), (76, 77, 79, 81, 81, 81))
ROUNDS = 82


def write_coded(ref, value):
    rows = value.shape[0]
    top = jnp.maximum(jnp.max(jnp.abs(value), axis=0, keepdims=True), 1e-30)
    power = jnp.ceil(jnp.log2(top))
    coded = jnp.round(value * (jnp.exp2(-power) * TOP)).astype(jnp.int16)
    ref[0:rows, :] = coded[:, 0:128]
    ref[rows : 2 * rows, :] = coded[:, 128:256]
    first = lax.broadcasted_iota(jnp.int32, (16, 128), 0) < 8
    ref[2 * rows : 2 * rows + 16, :] = jnp.where(first, power[:, 0:128], power[:, 128:256]).astype(jnp.int16)


def restored(ref, rows):
    power = ref[2 * rows : 2 * rows + 16, :].astype(jnp.float32)
    scale = jnp.exp2(power) * (1.0 / TOP)
    return jnp.concatenate(
        [ref[0:rows, :].astype(jnp.float32) * scale[0:1], ref[rows : 2 * rows, :].astype(jnp.float32) * scale[8:9]],
        axis=1,
    )


def kernel(
    ls, rs, kept, xr0, xr1, lbuf, rbuf, own, tot, val, hs, hr, zs, zr, xs0, xs1,
    la_s, la_r, ld_s, ld_r, lr_s, lr_r, dd_s, dd_r,
    ra_s, ra_r, rd_s, rd_r, rr_s, rr_r, h_s, h_r, z_s, z_r, x0_s, x0_r, x1_s, x1_r,
):
    row, core, z = lax.axis_index("row"), lax.axis_index("col"), lax.axis_index("rep")
    y, x = row // 4, row % 4

    def at_x(d):
        return (y * 4 + (x + d) % 4, core, z)

    def at_y(d):
        return ((y + d) % 4 * 4 + x, core, z)

    def at_z(d):
        return (row, core, (z + d) % 4)

    partner = (row, 1 - core, z)
    everyone = [f(d) for f in (at_x, at_y, at_z) for d in (1, 2, 3)] + [partner]

    def remote(src, dst, send, recv, device):
        return pltpu.make_async_remote_copy(
            src_ref=src, dst_ref=dst, send_sem=send, recv_sem=recv, device_id=device, device_id_type=MESH
        )

    def arrived(ref, sem):
        pltpu.make_async_copy(ref, ref, sem).wait()

    def rel_of(p):
        return jnp.where(p < 2, p, 5 - p)

    def y_at(p):
        return (y + rel_of(p)) % 4

    def lpiece(yy, xx, first=0, rows=96, side=None):
        side = core if side is None else side
        return lbuf.at[yy * 4 + xx, :, pl.ds(pl.multiple_of(side * 96 + first, 16), rows), :]

    def la_copy(d):
        return remote(ls.at[(y + d) % 4], lpiece(y, x), la_s.at[d - 1], la_r.at[4 - d], at_y(d))

    def la_local():
        return pltpu.make_async_copy(ls.at[y], lpiece(y, x), la_r.at[0])

    def ld_copy(p, way):
        ref = lpiece(y_at(p), x)
        return remote(ref, ref, ld_s.at[p, way], ld_r.at[p, way], at_x(1 if way == 0 else 3))

    def lr_copy(p, way):
        ref = lpiece(y_at(p), (x + (3 if way == 0 else 1)) % 4, 48 * way, 48)
        return remote(ref, ref, lr_s.at[p, way], lr_r.at[p, way], at_x(1 if way == 0 else 3))

    def dd_copy(p, xr):
        ref = lpiece(y_at(p), (x + xr) % 4)
        return remote(ref, ref, dd_s.at[p, xr], dd_r.at[p, xr], partner)

    def rpiece(s, xx):
        return rbuf.at[s, :, pl.ds(pl.multiple_of((y * 4 + xx) * 48, 16), 48), :]

    def rblock(s, yy, k0=0, nk=4):
        return rbuf.at[s, pl.ds(k0, nk), pl.ds(pl.multiple_of(yy * 192, 16), 192), :]

    def ra_copy(s, d):
        return remote(rs.at[(x + d) % 4, s], rpiece(s, x), ra_s.at[s, d - 1], ra_r.at[s, 4 - d], at_x(d))

    def ra_local(s):
        return pltpu.make_async_copy(rs.at[x, s], rpiece(s, x), ra_r.at[s, 0])

    def rd_copy(s, way):
        ref = rblock(s, y)
        return remote(ref, ref, rd_s.at[s, way], rd_r.at[s, way], at_y(1 if way == 0 else 3))

    def rr_copy(s, way):
        ref = rblock(s, (y + (3 if way == 0 else 1)) % 4, 2 * way, 2)
        return remote(ref, ref, rr_s.at[s, way], rr_r.at[s, way], at_y(1 if way == 0 else 3))

    def h_copy(xr, s, way):
        return remote(
            hs.at[xr, s, way], hr.at[xr, s, way], h_s.at[xr, s, way], h_r.at[xr, s, way], at_z(1 if way == 0 else 3)
        )

    def z_copy(way, xr, s):
        return remote(
            zs.at[way, xr, s], zr.at[way, xr, s], z_s.at[way, xr, s], z_r.at[way, xr, s], at_z(1 + 2 * way)
        )

    def x0_copy(s, d):
        return remote(xs0.at[s, d - 1], xr0.at[s, d - 1], x0_s.at[s, d - 1], x0_r.at[s, d - 1], at_x(d))

    def x1_copy(s, d):
        return remote(xs1.at[s, d - 1], xr1.at[s, d - 1], x1_s.at[s, d - 1], x1_r.at[s, d - 1], at_x(d))

    def ra_start(s):
        for d in (1, 3, 2):
            ra_copy(s, d).start()

    def ra_wait(s):
        for d in range(4):
            arrived(rpiece(s, (x + d) % 4), ra_r.at[s, d])

    def rd_start(s):
        for way in (0, 1):
            rd_copy(s, way).start()

    def rd_wait(s):
        for way in (0, 1):
            arrived(rblock(s, (y + (3 if way == 0 else 1)) % 4), rd_r.at[s, way])

    def rr_start(s):
        for way in (0, 1):
            rr_copy(s, way).start()

    def rr_wait(s):
        for way in (0, 1):
            arrived(rblock(s, (y + 2) % 4, 2 * way, 2), rr_r.at[s, way])

    def la_wait(p):
        d = rel_of(p)
        arrived(lpiece(y_at(p), x), la_r.at[d])
        dd_copy(p, 0).start()

    def ld_start(p):
        for way in (0, 1):
            ld_copy(p, way).start()

    def ld_wait(p):
        for way in (0, 1):
            xr = 3 if way == 0 else 1
            arrived(lpiece(y_at(p), (x + xr) % 4), ld_r.at[p, way])
            dd_copy(p, xr).start()

    def lr_start(p):
        for way in (0, 1):
            lr_copy(p, way).start()

    def lr_done(p):
        for way in (0, 1):
            arrived(lpiece(y_at(p), (x + 2) % 4, 48 * way, 48), lr_r.at[p, way])
        dd_copy(p, 2).start()

    def dd_wait(p, xr):
        arrived(lpiece(y_at(p), (x + xr) % 4, side=1 - core), dd_r.at[p, xr])

    def product(p, pieces, s):
        left = jnp.concatenate(
            [
                jnp.concatenate([lbuf[y_at(p) * 4 + (x + xr) % 4, k] for k in range(4)], axis=1)
                for xr in pieces
            ],
            axis=0,
        )
        return jnp.dot(left, rbuf[s].reshape(3072, NB), preferred_element_type=jnp.float32)

    def give_on(value, off, xr, s):
        @pl.when(off == 0)
        def _():
            own[s, xr] = value

        @pl.when(off == 2)
        def _():
            for way in (0, 1):
                write_coded(hs.at[xr, s, way], value[HROWS * way : HROWS * (way + 1)])
                h_copy(xr, s, way).start()

        for way in (0, 1):

            @pl.when(off == 1 + 2 * way)
            def _(way=way):
                arrived(hr.at[xr, s, way], h_r.at[xr, s, way])
                more = restored(hr.at[xr, s, way], HROWS)
                first, second = value[0:HROWS], value[HROWS:QROWS]
                if way == 0:
                    first = first + more
                else:
                    second = second + more
                write_coded(zs.at[way, xr, s], jnp.concatenate([first, second], axis=0))
                z_copy(way, xr, s).start()

    barrier = pltpu.get_barrier_semaphore()
    for device in everyone:
        pl.semaphore_signal(barrier, inc=1, device_id=device, device_id_type=MESH)
    pl.semaphore_wait(barrier, len(everyone))

    la_local().start()
    for s in range(NS):
        ra_local(s).start()

    does = {
        "ra": ra_start, "rd": rd_start, "rr": rr_start, "ld": ld_start, "lr": lr_start,
        "la": lambda d: la_copy(d).start(),
        "RA": ra_wait, "RD": rd_wait, "RR": rr_wait, "LA": la_wait, "LD": ld_wait, "LR": lr_done,
        "DD": lambda k: [dd_wait(k[0], xr) for xr in ((0,), (1, 3), (2,))[k[1]]],
    }

    def look(i):
        codes = [p * 32 + kind * 8 + s for p, kind, s in BLOCKS]
        word = 0
        for n in range(0, len(codes), 4):
            word = jnp.where(i // 4 == n // 4, sum(c * 128**m for m, c in enumerate(codes[n : n + 4])), word)
        m = i % 4
        shift = jnp.where(m == 0, 1, jnp.where(m == 1, 128, jnp.where(m == 2, 128**2, 128**3)))
        code = word // shift % 128
        return (i >= 0) & (i < len(codes)), code // 32, code // 8 % 4, code % 8

    def reduce(s, part):
        pieces = PARTS[part]
        sent, begin = (xs0, x0_copy) if part == 0 else (xs1, x1_copy)
        for xr in pieces:
            total = own[s, xr]
            for way in (0, 1):
                arrived(zr.at[way, xr, s], z_r.at[way, xr, s])
                total = total + restored(zr.at[way, xr, s], QROWS)
            tot[xr] = total

        def rows_of(i):
            return [
                tot[xr, pl.ds(pl.multiple_of(side * 96 + i * 24, 8), 24), :] for xr in pieces for side in range(2)
            ]

        def give(d, carry):
            write_coded(sent.at[s, d - 1], jnp.concatenate(rows_of((x + d) % 4), axis=0))
            begin(s, d).start()
            return carry

        lax.fori_loop(1, 4, give, 0)
        own_rows = rows_of(x)
        for n, xr in enumerate(pieces):
            kept[s, xr] = jnp.concatenate(own_rows[2 * n : 2 * n + 2], axis=0)

    def round_(i, carry):
        def events(n):
            todo = [(what, k) for m, what, k in EVENTS if m == n]
            if todo:

                @pl.when(i == n)
                def _():
                    for what, k in todo:
                        does[what](k)

        for g in range(0, len(BLOCKS), 9):
            if any(g <= m < g + 9 for m, _, _ in EVENTS):

                @pl.when((i >= g) & (i < g + 9))
                def _(g=g):
                    for n in range(g, g + 9):
                        events(n)

        def half(j, carry):
            there, p, kind, s = look(i - LAG * j)
            off = (y_at(p) - z + 4) % 4

            @pl.when(there & (off % 2 == j))
            def _():
                @pl.when(kind == 1)
                def _():
                    val[...] = product(p, (1, 3), s).reshape(2, QROWS, NB)

                @pl.when(kind != 1)
                def _():
                    val[0] = product(p, (kind,), s)

                def one(n, carry):
                    give_on(val[n], off, jnp.where(kind == 1, 1 + 2 * n, kind), s)
                    return carry

                lax.fori_loop(0, jnp.where(kind == 1, 2, 1), one, 0)

            return carry

        lax.fori_loop(0, 2, half, 0)

        for part in range(2):

            def sums(s, carry, part=part):
                reduce(s, part)
                return carry

            begun = sum(jnp.where(i > n, 1, 0) for n in SUMS[part])
            lax.fori_loop(begun, sum(jnp.where(i >= n, 1, 0) for n in SUMS[part]), sums, 0)
        return carry

    lax.fori_loop(0, ROUNDS, round_, 0)

    for d in (1, 2, 3):
        la_copy(d).wait_send()

    def sent_right(s, carry):
        for d in (1, 2, 3):
            ra_copy(s, d).wait_send()
        for way in (0, 1):
            rd_copy(s, way).wait_send()
            rr_copy(s, way).wait_send()
        return carry

    def sent_left(q, carry):
        for way in (0, 1):
            ld_copy(q, way).wait_send()
            lr_copy(q, way).wait_send()
        for xr in range(4):
            dd_copy(q, xr).wait_send()
        return carry

    def sent_z(n, carry):
        for way in (0, 1):
            h_copy(n // 6, n % 6, way).wait_send()
            z_copy(way, n // 6, n % 6).wait_send()
        return carry

    lax.fori_loop(0, NS, sent_right, 0)
    lax.fori_loop(0, 4, sent_left, 0)
    lax.fori_loop(0, 24, sent_z, 0)

    def finish(s, carry):
        for d in (1, 2, 3):
            arrived(xr0.at[s, d - 1], x0_r.at[s, d - 1])
            arrived(xr1.at[s, d - 1], x1_r.at[s, d - 1])
            x0_copy(s, d).wait_send()
            x1_copy(s, d).wait_send()
        return carry

    lax.fori_loop(0, NS, finish, 0)


def place_kernel(kept, came0, came1, out):
    x = lax.axis_index("row") % 4
    for bt in range(3):
        for d in range(4):
            source = (x - d + 4) % 4
            if d:
                first, last = restored(came0.at[bt, d - 1], 144), restored(came1.at[bt, d - 1], 48)
            for n, xr in enumerate((0, 1, 3, 2)):
                value = kept[bt, xr] if d == 0 else last if xr == 2 else first[48 * n : 48 * n + 48]
                at = pl.multiple_of((source + xr) % 4 * 48, 8)
                out[0, source, 0, pl.ds(at, 48), bt * NB : bt * NB + NB] = value


def right_kernel(mask, w, rs):
    k = pl.program_id(0)
    first = lax.axis_index("row") * 48
    tile = first // TILE
    after = jnp.minimum(tile + 1, 5)
    edge = (tile + 1) * TILE - first
    upper = lax.broadcasted_iota(jnp.int32, (48, TILE), 0) < edge
    rows = jnp.swapaxes(w[0], 0, 1)
    for j in range(8):
        for b in range(6):
            kept = jnp.where(upper, mask[k, tile, j, b].astype(jnp.float32), mask[k, after, j, b].astype(jnp.float32))
            rs[j // 2, j % 2 * 3 + b // 2, 0, :, b % 2 * TILE : (b % 2 + 1) * TILE] = (
                rows[j, :, b * TILE : (b + 1) * TILE] * kept.astype(jnp.bfloat16)
            )


def on_device(amplitudes, integrals, pair_mask, tile_mask):
    kept = amplitudes * pair_mask[:, :, None, None].astype(jnp.bfloat16)
    ls = kept.reshape(4, 4, 4, 24, 768).transpose(0, 2, 1, 3, 4).reshape(4, 4, 96, 768)
    rs = pl.pallas_call(
        right_kernel,
        grid=(4,),
        out_shape=jax.ShapeDtypeStruct((4, NS, 4, 48, NB), jnp.bfloat16),
        in_specs=[
            pl.BlockSpec(memory_space=pltpu.SMEM),
            pl.BlockSpec((1, 48, 8, 768), lambda k: (k, 0, 0, 0)),
        ],
        out_specs=pl.BlockSpec((4, NS, 1, 48, NB), lambda k: (0, 0, k, 0, 0)),
        cost_estimate=pl.CostEstimate(flops=10**6, bytes_accessed=5 * 10**6, transcendentals=0),
    )(tile_mask, integrals)
    dma = pltpu.SemaphoreType.DMA
    bf, i16, f32 = jnp.bfloat16, jnp.int16, jnp.float32
    came = ((NS, 3) + coded_shape(144), (NS, 3) + coded_shape(48))
    parts = pl.pallas_call(
        kernel,
        out_shape=(
            jax.ShapeDtypeStruct((NS, 4, 48, NB), f32),
            jax.ShapeDtypeStruct(came[0], i16),
            jax.ShapeDtypeStruct(came[1], i16),
        ),
        in_specs=[pl.BlockSpec(memory_space=pl.ANY)] * 2,
        out_specs=[pl.BlockSpec(memory_space=pltpu.VMEM)] * 3,
        scratch_shapes=[
            pltpu.VMEM((16, 4, 192, 768), bf),
            pltpu.VMEM((NS, 4, 768, NB), bf),
            pltpu.VMEM((NS, 4, QROWS, NB), f32),
            pltpu.VMEM((4, QROWS, NB), f32),
            pltpu.VMEM((2, QROWS, NB), f32),
            pltpu.VMEM((4, NS, 2) + coded_shape(HROWS), i16),
            pltpu.VMEM((4, NS, 2) + coded_shape(HROWS), i16),
            pltpu.VMEM((2, 4, NS) + coded_shape(QROWS), i16),
            pltpu.VMEM((2, 4, NS) + coded_shape(QROWS), i16),
            pltpu.VMEM((NS, 3) + coded_shape(144), i16),
            pltpu.VMEM((NS, 3) + coded_shape(48), i16),
            dma((3,)), dma((4,)), dma((4, 2)), dma((4, 2)), dma((4, 2)), dma((4, 2)), dma((4, 4)), dma((4, 4)),
            dma((NS, 3)), dma((NS, 4)), dma((NS, 2)), dma((NS, 2)), dma((NS, 2)), dma((NS, 2)),
            dma((4, NS, 2)), dma((4, NS, 2)), dma((2, 4, NS)), dma((2, 4, NS)), dma((NS, 3)), dma((NS, 3)),
            dma((NS, 3)), dma((NS, 3)),
        ],
        compiler_params=pltpu.CompilerParams(
            collective_id=0, has_side_effects=True, vmem_limit_bytes=63 * 2**20
        ),
        cost_estimate=pl.CostEstimate(flops=29 * 10**9, bytes_accessed=10**7, transcendentals=0),
    )(ls, rs)
    done = pl.pallas_call(
        place_kernel,
        grid=(2,),
        out_shape=jax.ShapeDtypeStruct((1, 4, 2, QROWS, 768), f32),
        in_specs=[
            pl.BlockSpec((3, 4, 48, NB), lambda s: (s, 0, 0, 0)),
            pl.BlockSpec((3,) + came[0][1:], lambda s: (s, 0, 0, 0)),
            pl.BlockSpec((3,) + came[1][1:], lambda s: (s, 0, 0, 0)),
        ],
        out_specs=pl.BlockSpec((1, 4, 1, QROWS, 768), lambda s: (0, 0, s, 0, 0)),
        cost_estimate=pl.CostEstimate(flops=10**7, bytes_accessed=8 * 10**6, transcendentals=0),
    )(*parts)
    return done.reshape(1, 8, QROWS, 768)


def solution(mesh):
    placed = (
        P(None, "rep", ("row", "col"), None),
        P("rep", "row", "col", None),
        P(None, "rep"),
        P("rep", None, "col", None),
    )
    return jax.shard_map(
        on_device,
        mesh=mesh,
        in_specs=placed,
        out_specs=P("row", "col", "rep", None),
        check_vma=False,
    )
```

```python
import jax
import jax.numpy as jnp
from jax import lax
from jax.experimental import pallas as pl
from jax.experimental.pallas import tpu as pltpu
from jax.sharding import PartitionSpec as P

TILE = 128
MESH = pl.DeviceIdType.MESH
NS = 6
NB = 256
QROWS = 192
HROWS = 96


def coded_shape(rows):
    return (2 * rows + 16, 128)


PARTS = ((0, 1, 3), (2,))
TOP = 32766.0
ROUND = 12582912.0


EVENTS = (
    (0, "ra", 0), (0, "ra", 1), (0, "ra", 2), (0, "LA", 0), (0, "ra", 3), (0, "la", 1), (0, "la", 3),
    (0, "RA", 0), (0, "rd", 0), (0, "RA", 1), (0, "RA", 2), (0, "LA", 2), (0, "LA", 1), (0, "ld", 1),
    (0, "ld", 2), (0, "ld", 0), (0, "RA", 3), (0, "RD", 0), (0, "rr", 0), (0, "la", 2), (0, "rd", 1),
    (0, "rd", 2), (0, "RR", 0), (0, "DD", (0, 0)), (1, "DD", (1, 0)), (2, "LD", 1), (2, "DD", (2, 0)),
    (3, "DD", (1, 1)), (4, "LA", 3), (4, "ld", 3), (4, "ra", 4), (4, "LD", 2), (4, "lr", 2),
    (4, "DD", (3, 0)), (5, "DD", (2, 1)), (6, "RD", 1), (6, "rr", 1), (6, "rd", 3), (6, "LD", 0),
    (6, "lr", 0), (6, "ra", 5), (6, "lr", 1), (6, "RD", 2), (6, "rr", 2), (6, "DD", (0, 1)), (7, "RR", 1),
    (13, "LD", 3), (13, "lr", 3), (14, "RD", 3), (14, "rr", 3), (14, "RA", 4), (14, "rd", 4),
    (14, "DD", (3, 1)), (16, "RR", 2), (20, "LR", 2), (21, "RR", 3), (27, "LR", 0), (28, "RD", 4),
    (28, "rr", 4), (29, "RA", 5), (29, "rd", 5), (32, "RR", 4), (34, "LR", 1), (39, "LR", 3), (39, "RD", 5),
    (39, "rr", 5), (40, "DD", (0, 2)), (41, "DD", (1, 2)), (42, "DD", (2, 2)), (43, "DD", (3, 2)),
    (46, "RR", 5),
)
BLOCKS = (
    (0, 0, 0), (1, 0, 0), (2, 0, 0), (1, 1, 0), (3, 0, 0), (2, 1, 0), (0, 1, 0), (0, 0, 1), (1, 0, 1),
    (2, 0, 1), (3, 0, 1), (0, 1, 1), (1, 1, 1), (2, 1, 1), (3, 1, 0), (3, 1, 1), (0, 0, 2), (1, 0, 2),
    (2, 0, 2), (3, 0, 2), (0, 1, 2), (0, 0, 3), (1, 0, 3), (2, 0, 3), (3, 0, 3), (1, 1, 2), (2, 1, 2),
    (3, 1, 2), (0, 1, 3), (1, 1, 3), (2, 1, 3), (3, 1, 3), (0, 0, 4), (1, 0, 4), (2, 0, 4), (3, 0, 4),
    (0, 1, 4), (1, 1, 4), (2, 1, 4), (3, 1, 4), (0, 2, 0), (1, 2, 0), (2, 2, 0), (3, 2, 0), (0, 2, 1),
    (1, 2, 1), (0, 0, 5), (1, 0, 5), (2, 0, 5), (3, 0, 5), (0, 1, 5), (1, 1, 5), (2, 1, 5), (3, 1, 5),
    (2, 2, 1), (3, 2, 1), (0, 2, 2), (1, 2, 2), (2, 2, 2), (3, 2, 2), (0, 2, 3), (1, 2, 3), (2, 2, 3),
    (3, 2, 3), (0, 2, 4), (1, 2, 4), (2, 2, 4), (3, 2, 4), (0, 2, 5), (1, 2, 5), (2, 2, 5), (3, 2, 5),
)
LAG = 8
SUMS = ((45, 45, 45, 47, 55, 69), (69, 71, 75, 79, 79, 79))
ROUNDS = 80


def write_coded(ref, value):
    rows = value.shape[0]
    top = jnp.maximum(jnp.max(jnp.abs(value), axis=0, keepdims=True), 1e-30)
    power = jnp.ceil(jnp.log2(top))
    coded = ((value * (jnp.exp2(-power) * TOP) + ROUND) - ROUND).astype(jnp.int16)
    ref[0:rows, :] = coded[:, 0:128]
    ref[rows : 2 * rows, :] = coded[:, 128:256]
    first = lax.broadcasted_iota(jnp.int32, (16, 128), 0) < 8
    ref[2 * rows : 2 * rows + 16, :] = jnp.where(first, power[:, 0:128], power[:, 128:256]).astype(jnp.int16)


def restored(ref, rows):
    power = ref[2 * rows : 2 * rows + 16, :].astype(jnp.float32)
    scale = jnp.exp2(power) * (1.0 / TOP)
    return jnp.concatenate(
        [ref[0:rows, :].astype(jnp.float32) * scale[0:1], ref[rows : 2 * rows, :].astype(jnp.float32) * scale[8:9]],
        axis=1,
    )


def kernel(
    ls, rs, kept, xr0, xr1, lbuf, rbuf, own, tot, val, hs, hr, zs, zr, xs0, xs1,
    la_s, la_r, ld_s, ld_r, lr_s, lr_r, dd_s, dd_r,
    ra_s, ra_r, rd_s, rd_r, rr_s, rr_r, h_s, h_r, z_s, z_r, x0_s, x0_r, x1_s, x1_r,
):
    row, core, z = lax.axis_index("row"), lax.axis_index("col"), lax.axis_index("rep")
    y, x = row // 4, row % 4

    def at_x(d):
        return (y * 4 + (x + d) % 4, core, z)

    def at_y(d):
        return ((y + d) % 4 * 4 + x, core, z)

    def at_z(d):
        return (row, core, (z + d) % 4)

    partner = (row, 1 - core, z)
    everyone = [f(d) for f in (at_x, at_y, at_z) for d in (1, 2, 3)] + [partner]

    def remote(src, dst, send, recv, device):
        return pltpu.make_async_remote_copy(
            src_ref=src, dst_ref=dst, send_sem=send, recv_sem=recv, device_id=device, device_id_type=MESH
        )

    def arrived(ref, sem):
        pltpu.make_async_copy(ref, ref, sem).wait()

    def rel_of(p):
        return jnp.where(p < 2, p, 5 - p)

    def y_at(p):
        return (y + rel_of(p)) % 4

    def lpiece(yy, xx, first=0, rows=96, side=None):
        side = core if side is None else side
        return lbuf.at[yy * 4 + xx, :, pl.ds(pl.multiple_of(side * 96 + first, 16), rows), :]

    def la_copy(d):
        return remote(ls.at[(y + d) % 4], lpiece(y, x), la_s.at[d - 1], la_r.at[4 - d], at_y(d))

    def la_local():
        return pltpu.make_async_copy(ls.at[y], lpiece(y, x), la_r.at[0])

    def ld_copy(p, way):
        ref = lpiece(y_at(p), x)
        return remote(ref, ref, ld_s.at[p, way], ld_r.at[p, way], at_x(1 if way == 0 else 3))

    def lr_copy(p, way):
        ref = lpiece(y_at(p), (x + (3 if way == 0 else 1)) % 4, 48 * way, 48)
        return remote(ref, ref, lr_s.at[p, way], lr_r.at[p, way], at_x(1 if way == 0 else 3))

    def dd_copy(p, xr):
        ref = lpiece(y_at(p), (x + xr) % 4)
        return remote(ref, ref, dd_s.at[p, xr], dd_r.at[p, xr], partner)

    def rpiece(s, xx):
        return rbuf.at[s, :, pl.ds(pl.multiple_of((y * 4 + xx) * 48, 16), 48), :]

    def rblock(s, yy, k0=0, nk=4):
        return rbuf.at[s, pl.ds(k0, nk), pl.ds(pl.multiple_of(yy * 192, 16), 192), :]

    def ra_copy(s, d):
        return remote(rs.at[(x + d) % 4, s], rpiece(s, x), ra_s.at[s, d - 1], ra_r.at[s, 4 - d], at_x(d))

    def ra_local(s):
        return pltpu.make_async_copy(rs.at[x, s], rpiece(s, x), ra_r.at[s, 0])

    def rd_copy(s, way):
        ref = rblock(s, y)
        return remote(ref, ref, rd_s.at[s, way], rd_r.at[s, way], at_y(1 if way == 0 else 3))

    def rr_copy(s, way):
        ref = rblock(s, (y + (3 if way == 0 else 1)) % 4, 2 * way, 2)
        return remote(ref, ref, rr_s.at[s, way], rr_r.at[s, way], at_y(1 if way == 0 else 3))

    def h_copy(xr, s, way):
        return remote(
            hs.at[xr, s, way], hr.at[xr, s, way], h_s.at[xr, s, way], h_r.at[xr, s, way], at_z(1 if way == 0 else 3)
        )

    def z_copy(way, xr, s):
        return remote(
            zs.at[way, xr, s], zr.at[way, xr, s], z_s.at[way, xr, s], z_r.at[way, xr, s], at_z(1 + 2 * way)
        )

    def x0_copy(s, d):
        return remote(xs0.at[s, d - 1], xr0.at[s, d - 1], x0_s.at[s, d - 1], x0_r.at[s, d - 1], at_x(d))

    def x1_copy(s, d):
        return remote(xs1.at[s, d - 1], xr1.at[s, d - 1], x1_s.at[s, d - 1], x1_r.at[s, d - 1], at_x(d))

    def ra_start(s):
        for d in (1, 3, 2):
            ra_copy(s, d).start()

    def ra_wait(s):
        for d in range(4):
            arrived(rpiece(s, (x + d) % 4), ra_r.at[s, d])

    def rd_start(s):
        for way in (0, 1):
            rd_copy(s, way).start()

    def rd_wait(s):
        for way in (0, 1):
            arrived(rblock(s, (y + (3 if way == 0 else 1)) % 4), rd_r.at[s, way])

    def rr_start(s):
        for way in (0, 1):
            rr_copy(s, way).start()

    def rr_wait(s):
        for way in (0, 1):
            arrived(rblock(s, (y + 2) % 4, 2 * way, 2), rr_r.at[s, way])

    def la_wait(p):
        d = rel_of(p)
        arrived(lpiece(y_at(p), x), la_r.at[d])
        dd_copy(p, 0).start()

    def ld_start(p):
        for way in (0, 1):
            ld_copy(p, way).start()

    def ld_wait(p):
        for way in (0, 1):
            xr = 3 if way == 0 else 1
            arrived(lpiece(y_at(p), (x + xr) % 4), ld_r.at[p, way])
            dd_copy(p, xr).start()

    def lr_start(p):
        for way in (0, 1):
            lr_copy(p, way).start()

    def lr_done(p):
        for way in (0, 1):
            arrived(lpiece(y_at(p), (x + 2) % 4, 48 * way, 48), lr_r.at[p, way])
        dd_copy(p, 2).start()

    def dd_wait(p, xr):
        arrived(lpiece(y_at(p), (x + xr) % 4, side=1 - core), dd_r.at[p, xr])

    def product(p, pieces, s):
        left = jnp.concatenate(
            [
                jnp.concatenate([lbuf[y_at(p) * 4 + (x + xr) % 4, k] for k in range(4)], axis=1)
                for xr in pieces
            ],
            axis=0,
        )
        return jnp.dot(left, rbuf[s].reshape(3072, NB), preferred_element_type=jnp.float32)

    def give_on(value, off, xr, s):
        @pl.when(off == 0)
        def _():
            own[s, xr] = value

        @pl.when(off == 2)
        def _():
            for way in (0, 1):
                write_coded(hs.at[xr, s, way], value[HROWS * way : HROWS * (way + 1)])
                h_copy(xr, s, way).start()

        for way in (0, 1):

            @pl.when(off == 1 + 2 * way)
            def _(way=way):
                arrived(hr.at[xr, s, way], h_r.at[xr, s, way])
                more = restored(hr.at[xr, s, way], HROWS)
                first, second = value[0:HROWS], value[HROWS:QROWS]
                if way == 0:
                    first = first + more
                else:
                    second = second + more
                write_coded(zs.at[way, xr, s], jnp.concatenate([first, second], axis=0))
                z_copy(way, xr, s).start()

    barrier = pltpu.get_barrier_semaphore()
    for device in everyone:
        pl.semaphore_signal(barrier, inc=1, device_id=device, device_id_type=MESH)
    pl.semaphore_wait(barrier, len(everyone))

    la_local().start()
    for s in range(NS):
        ra_local(s).start()

    does = {
        "ra": ra_start, "rd": rd_start, "rr": rr_start, "ld": ld_start, "lr": lr_start,
        "la": lambda d: la_copy(d).start(),
        "RA": ra_wait, "RD": rd_wait, "RR": rr_wait, "LA": la_wait, "LD": ld_wait, "LR": lr_done,
        "DD": lambda k: [dd_wait(k[0], xr) for xr in ((0,), (1, 3), (2,))[k[1]]],
    }

    def look(i):
        codes = [p * 32 + kind * 8 + s for p, kind, s in BLOCKS]
        word = 0
        for n in range(0, len(codes), 4):
            word = jnp.where(i // 4 == n // 4, sum(c * 128**m for m, c in enumerate(codes[n : n + 4])), word)
        m = i % 4
        shift = jnp.where(m == 0, 1, jnp.where(m == 1, 128, jnp.where(m == 2, 128**2, 128**3)))
        code = word // shift % 128
        return (i >= 0) & (i < len(codes)), code // 32, code // 8 % 4, code % 8

    def reduce(s, part):
        pieces = PARTS[part]
        sent, begin = (xs0, x0_copy) if part == 0 else (xs1, x1_copy)
        for xr in pieces:
            total = own[s, xr]
            for way in (0, 1):
                arrived(zr.at[way, xr, s], z_r.at[way, xr, s])
                total = total + restored(zr.at[way, xr, s], QROWS)
            tot[xr] = total

        def rows_of(i):
            return [
                tot[xr, pl.ds(pl.multiple_of(side * 96 + i * 24, 8), 24), :] for xr in pieces for side in range(2)
            ]

        def give(d, carry):
            write_coded(sent.at[s, d - 1], jnp.concatenate(rows_of((x + d) % 4), axis=0))
            begin(s, d).start()
            return carry

        lax.fori_loop(1, 4, give, 0)
        own_rows = rows_of(x)
        for n, xr in enumerate(pieces):
            kept[s, xr] = jnp.concatenate(own_rows[2 * n : 2 * n + 2], axis=0)

    def round_(i, carry):
        def events(n):
            todo = [(what, k) for m, what, k in EVENTS if m == n]
            if todo:

                @pl.when(i == n)
                def _():
                    for what, k in todo:
                        does[what](k)

        for g in range(0, len(BLOCKS), 9):
            if any(g <= m < g + 9 for m, _, _ in EVENTS):

                @pl.when((i >= g) & (i < g + 9))
                def _(g=g):
                    for n in range(g, g + 9):
                        events(n)

        def half(j, carry):
            there, p, kind, s = look(i - LAG * j)
            off = (y_at(p) - z + 4) % 4

            @pl.when(there & (off % 2 == j))
            def _():
                @pl.when(kind == 1)
                def _():
                    val[...] = product(p, (1, 3), s).reshape(2, QROWS, NB)

                @pl.when(kind != 1)
                def _():
                    val[0] = product(p, (kind,), s)

                def one(n, carry):
                    give_on(val[n], off, jnp.where(kind == 1, 1 + 2 * n, kind), s)
                    return carry

                lax.fori_loop(0, jnp.where(kind == 1, 2, 1), one, 0)

            return carry

        lax.fori_loop(0, 2, half, 0)

        for part in range(2):

            def sums(s, carry, part=part):
                reduce(s, part)
                return carry

            begun = sum(jnp.where(i > n, 1, 0) for n in SUMS[part])
            lax.fori_loop(begun, sum(jnp.where(i >= n, 1, 0) for n in SUMS[part]), sums, 0)
        return carry

    lax.fori_loop(0, ROUNDS, round_, 0)

    for d in (1, 2, 3):
        la_copy(d).wait_send()

    def sent_right(s, carry):
        for d in (1, 2, 3):
            ra_copy(s, d).wait_send()
        for way in (0, 1):
            rd_copy(s, way).wait_send()
            rr_copy(s, way).wait_send()
        return carry

    def sent_left(q, carry):
        for way in (0, 1):
            ld_copy(q, way).wait_send()
            lr_copy(q, way).wait_send()
        for xr in range(4):
            dd_copy(q, xr).wait_send()
        return carry

    def sent_z(n, carry):
        for way in (0, 1):
            h_copy(n // 6, n % 6, way).wait_send()
            z_copy(way, n // 6, n % 6).wait_send()
        return carry

    lax.fori_loop(0, NS, sent_right, 0)
    lax.fori_loop(0, 4, sent_left, 0)
    lax.fori_loop(0, 24, sent_z, 0)

    def finish(s, carry):
        for d in (1, 2, 3):
            arrived(xr0.at[s, d - 1], x0_r.at[s, d - 1])
            arrived(xr1.at[s, d - 1], x1_r.at[s, d - 1])
            x0_copy(s, d).wait_send()
            x1_copy(s, d).wait_send()
        return carry

    lax.fori_loop(0, NS, finish, 0)


def place_kernel(kept, came0, came1, out):
    x = lax.axis_index("row") % 4
    for bt in range(3):
        for d in range(4):
            source = (x - d + 4) % 4
            if d:
                first, last = restored(came0.at[bt, d - 1], 144), restored(came1.at[bt, d - 1], 48)
            for n, xr in enumerate((0, 1, 3, 2)):
                value = kept[bt, xr] if d == 0 else last if xr == 2 else first[48 * n : 48 * n + 48]
                at = pl.multiple_of((source + xr) % 4 * 48, 8)
                out[0, source, 0, pl.ds(at, 48), bt * NB : bt * NB + NB] = value


def right_kernel(mask, w, rs):
    first = lax.axis_index("row") * 48
    tile = first // TILE
    after = jnp.minimum(tile + 1, 5)
    edge = (tile + 1) * TILE - first
    upper = lax.broadcasted_iota(jnp.int32, (48, TILE), 0) < edge
    rows = jnp.swapaxes(w[0], 0, 1)
    low, high = mask[0, tile].astype(jnp.float32), mask[0, after].astype(jnp.float32)
    for j in range(8):
        for b in range(6):
            kept = jnp.where(upper, low[j : j + 1, b : b + 1], high[j : j + 1, b : b + 1])
            rs[j // 2, j % 2 * 3 + b // 2, 0, :, b % 2 * TILE : (b % 2 + 1) * TILE] = (
                rows[j, :, b * TILE : (b + 1) * TILE] * kept.astype(jnp.bfloat16)
            )


def on_device(amplitudes, integrals, pair_mask, tile_mask):
    kept = jnp.where(pair_mask[:, :, None, None] != 0, amplitudes, jnp.zeros((), jnp.bfloat16))
    ls = kept.reshape(4, 4, 4, 24, 768).transpose(0, 2, 1, 3, 4).reshape(4, 4, 96, 768)
    rs = pl.pallas_call(
        right_kernel,
        grid=(4,),
        out_shape=jax.ShapeDtypeStruct((4, NS, 4, 48, NB), jnp.bfloat16),
        in_specs=[
            pl.BlockSpec((1, 6, 8, 6), lambda k: (k, 0, 0, 0)),
            pl.BlockSpec((1, 48, 8, 768), lambda k: (k, 0, 0, 0)),
        ],
        out_specs=pl.BlockSpec((4, NS, 1, 48, NB), lambda k: (0, 0, k, 0, 0)),
        cost_estimate=pl.CostEstimate(flops=10**6, bytes_accessed=5 * 10**6, transcendentals=0),
    )(tile_mask, integrals)
    dma = pltpu.SemaphoreType.DMA
    bf, i16, f32 = jnp.bfloat16, jnp.int16, jnp.float32
    came = ((NS, 3) + coded_shape(144), (NS, 3) + coded_shape(48))
    parts = pl.pallas_call(
        kernel,
        out_shape=(
            jax.ShapeDtypeStruct((NS, 4, 48, NB), f32),
            jax.ShapeDtypeStruct(came[0], i16),
            jax.ShapeDtypeStruct(came[1], i16),
        ),
        in_specs=[pl.BlockSpec(memory_space=pl.ANY)] * 2,
        out_specs=[pl.BlockSpec(memory_space=pltpu.VMEM)] * 3,
        scratch_shapes=[
            pltpu.VMEM((16, 4, 192, 768), bf),
            pltpu.VMEM((NS, 4, 768, NB), bf),
            pltpu.VMEM((NS, 4, QROWS, NB), f32),
            pltpu.VMEM((4, QROWS, NB), f32),
            pltpu.VMEM((2, QROWS, NB), f32),
            pltpu.VMEM((4, NS, 2) + coded_shape(HROWS), i16),
            pltpu.VMEM((4, NS, 2) + coded_shape(HROWS), i16),
            pltpu.VMEM((2, 4, NS) + coded_shape(QROWS), i16),
            pltpu.VMEM((2, 4, NS) + coded_shape(QROWS), i16),
            pltpu.VMEM((NS, 3) + coded_shape(144), i16),
            pltpu.VMEM((NS, 3) + coded_shape(48), i16),
            dma((3,)), dma((4,)), dma((4, 2)), dma((4, 2)), dma((4, 2)), dma((4, 2)), dma((4, 4)), dma((4, 4)),
            dma((NS, 3)), dma((NS, 4)), dma((NS, 2)), dma((NS, 2)), dma((NS, 2)), dma((NS, 2)),
            dma((4, NS, 2)), dma((4, NS, 2)), dma((2, 4, NS)), dma((2, 4, NS)), dma((NS, 3)), dma((NS, 3)),
            dma((NS, 3)), dma((NS, 3)),
        ],
        compiler_params=pltpu.CompilerParams(
            collective_id=0, has_side_effects=True, vmem_limit_bytes=63 * 2**20
        ),
        cost_estimate=pl.CostEstimate(flops=29 * 10**9, bytes_accessed=10**7, transcendentals=0),
    )(ls, rs)
    done = pl.pallas_call(
        place_kernel,
        grid=(2,),
        out_shape=jax.ShapeDtypeStruct((1, 4, 2, QROWS, 768), f32),
        in_specs=[
            pl.BlockSpec((3, 4, 48, NB), lambda s: (s, 0, 0, 0)),
            pl.BlockSpec((3,) + came[0][1:], lambda s: (s, 0, 0, 0)),
            pl.BlockSpec((3,) + came[1][1:], lambda s: (s, 0, 0, 0)),
        ],
        out_specs=pl.BlockSpec((1, 4, 1, QROWS, 768), lambda s: (0, 0, s, 0, 0)),
        cost_estimate=pl.CostEstimate(flops=10**7, bytes_accessed=8 * 10**6, transcendentals=0),
    )(*parts)
    return done.reshape(1, 8, QROWS, 768)


def solution(mesh):
    placed = (
        P(None, "rep", ("row", "col"), None),
        P("rep", "row", "col", None),
        P(None, "rep"),
        P("rep", None, "col", None),
    )
    return jax.shard_map(
        on_device,
        mesh=mesh,
        in_specs=placed,
        out_specs=P("row", "col", "rep", None),
        check_vma=False,
    )
```

```python
import jax
import jax.numpy as jnp
from jax import lax
from jax.experimental import pallas as pl
from jax.experimental.pallas import tpu as pltpu
from jax.sharding import PartitionSpec as P

TILE = 128
MESH = pl.DeviceIdType.MESH
NS = 6
NB = 256
QROWS = 192
HROWS = 96


def coded_shape(rows):
    return (2 * rows + 16, 128)


PARTS = ((0, 1, 3), (2,))
TOP = 32766.0
ROUND = 12582912.0


EVENTS = (
    (0, "ra", 0), (0, "ra", 1), (0, "ra", 2), (0, "LA", 0), (0, "ld", 0), (0, "la", 3), (0, "la", 1),
    (0, "RA", 0), (0, "rd", 0), (0, "LA", 1), (0, "LA", 2), (0, "ld", 2), (0, "ra", 3), (0, "ld", 1),
    (0, "ra", 4), (0, "LD", 0), (0, "RA", 1), (0, "rd", 1), (0, "RD", 0), (0, "rr", 0), (0, "la", 2),
    (0, "RA", 2), (0, "rd", 2), (0, "RD", 1), (0, "rr", 1), (0, "RR", 0), (0, "DD", (0, 0)),
    (1, "DD", (1, 0)), (2, "DD", (2, 0)), (3, "LD", 2), (3, "DD", (0, 1)), (4, "RA", 3), (4, "rd", 3),
    (4, "DD", (2, 1)), (5, "LA", 3), (5, "ld", 3), (5, "lr", 2), (5, "ra", 5), (5, "DD", (3, 0)),
    (6, "LD", 1), (6, "lr", 1), (6, "lr", 0), (6, "RD", 2), (6, "rr", 2), (6, "RA", 4), (6, "DD", (1, 1)),
    (7, "RR", 1), (14, "RD", 3), (14, "rr", 3), (14, "rd", 4), (14, "LD", 3), (14, "lr", 3), (14, "RR", 2),
    (18, "DD", (3, 1)), (19, "RR", 3), (19, "LR", 2), (24, "RA", 5), (27, "RD", 4), (27, "rr", 4),
    (27, "rd", 5), (28, "LR", 1), (31, "RR", 4), (33, "LR", 0), (38, "LR", 3), (38, "RD", 5), (38, "rr", 5),
    (40, "DD", (0, 2)), (41, "DD", (1, 2)), (42, "DD", (2, 2)), (43, "DD", (3, 2)), (44, "RR", 5),
)
BLOCKS = (
    (0, 0, 0), (1, 0, 0), (2, 0, 0), (0, 1, 0), (2, 1, 0), (3, 0, 0), (1, 1, 0), (0, 0, 1), (1, 0, 1),
    (2, 0, 1), (3, 0, 1), (0, 1, 1), (1, 1, 1), (2, 1, 1), (0, 0, 2), (1, 0, 2), (2, 0, 2), (3, 0, 2),
    (3, 1, 0), (0, 0, 3), (1, 0, 3), (2, 0, 3), (3, 0, 3), (3, 1, 1), (0, 1, 2), (1, 1, 2), (2, 1, 2),
    (3, 1, 2), (0, 1, 3), (1, 1, 3), (2, 1, 3), (0, 0, 4), (1, 0, 4), (2, 0, 4), (3, 0, 4), (3, 1, 3),
    (0, 1, 4), (1, 1, 4), (2, 1, 4), (3, 1, 4), (0, 2, 0), (1, 2, 0), (2, 2, 0), (3, 2, 0), (0, 0, 5),
    (1, 0, 5), (2, 0, 5), (3, 0, 5), (0, 1, 5), (1, 1, 5), (2, 1, 5), (3, 1, 5), (0, 2, 1), (1, 2, 1),
    (2, 2, 1), (3, 2, 1), (0, 2, 2), (1, 2, 2), (2, 2, 2), (3, 2, 2), (0, 2, 3), (1, 2, 3), (2, 2, 3),
    (3, 2, 3), (0, 2, 4), (1, 2, 4), (2, 2, 4), (3, 2, 4), (0, 2, 5), (1, 2, 5), (2, 2, 5), (3, 2, 5),
)
LAG = 6
SUMS = ((43, 43, 45, 53, 57, 69), (69, 73, 77, 77, 77, 77))
ROUNDS = 78


def write_coded(ref, value):
    rows = value.shape[0]
    top = jnp.maximum(jnp.max(jnp.abs(value), axis=0, keepdims=True), 1e-30)
    power = jnp.ceil(jnp.log2(top))
    coded = ((value * (jnp.exp2(-power) * TOP) + ROUND) - ROUND).astype(jnp.int16)
    ref[0:rows, :] = coded[:, 0:128]
    ref[rows : 2 * rows, :] = coded[:, 128:256]
    first = lax.broadcasted_iota(jnp.int32, (16, 128), 0) < 8
    ref[2 * rows : 2 * rows + 16, :] = jnp.where(first, power[:, 0:128], power[:, 128:256]).astype(jnp.int16)


def restored(ref, rows):
    power = ref[2 * rows : 2 * rows + 16, :].astype(jnp.float32)
    scale = jnp.exp2(power) * (1.0 / TOP)
    return jnp.concatenate(
        [ref[0:rows, :].astype(jnp.float32) * scale[0:1], ref[rows : 2 * rows, :].astype(jnp.float32) * scale[8:9]],
        axis=1,
    )


def kernel(
    ls, rs, kept, xr0, xr1, lbuf, rbuf, own, tot, val, hs, hr, zs, zr, xs0, xs1,
    la_s, la_r, ld_s, ld_r, lr_s, lr_r, dd_s, dd_r,
    ra_s, ra_r, rd_s, rd_r, rr_s, rr_r, h_s, h_r, z_s, z_r, x0_s, x0_r, x1_s, x1_r,
):
    row, core, z = lax.axis_index("row"), lax.axis_index("col"), lax.axis_index("rep")
    y, x = row // 4, row % 4

    def at_x(d):
        return (y * 4 + (x + d) % 4, core, z)

    def at_y(d):
        return ((y + d) % 4 * 4 + x, core, z)

    def at_z(d):
        return (row, core, (z + d) % 4)

    partner = (row, 1 - core, z)
    everyone = [f(d) for f in (at_x, at_y, at_z) for d in (1, 2, 3)] + [partner]

    def remote(src, dst, send, recv, device):
        return pltpu.make_async_remote_copy(
            src_ref=src, dst_ref=dst, send_sem=send, recv_sem=recv, device_id=device, device_id_type=MESH
        )

    def arrived(ref, sem):
        pltpu.make_async_copy(ref, ref, sem).wait()

    def rel_of(p):
        return jnp.where(p < 2, p, 5 - p)

    def y_at(p):
        return (y + rel_of(p)) % 4

    def lpiece(yy, xx, first=0, rows=96, side=None):
        side = core if side is None else side
        return lbuf.at[yy * 4 + xx, :, pl.ds(pl.multiple_of(side * 96 + first, 16), rows), :]

    def la_copy(d):
        return remote(ls.at[(y + d) % 4], lpiece(y, x), la_s.at[d - 1], la_r.at[4 - d], at_y(d))

    def la_local():
        return pltpu.make_async_copy(ls.at[y], lpiece(y, x), la_r.at[0])

    def ld_copy(p, way):
        ref = lpiece(y_at(p), x)
        return remote(ref, ref, ld_s.at[p, way], ld_r.at[p, way], at_x(1 if way == 0 else 3))

    def lr_copy(p, way):
        ref = lpiece(y_at(p), (x + (3 if way == 0 else 1)) % 4, 48 * way, 48)
        return remote(ref, ref, lr_s.at[p, way], lr_r.at[p, way], at_x(1 if way == 0 else 3))

    def dd_copy(p, xr):
        ref = lpiece(y_at(p), (x + xr) % 4)
        return remote(ref, ref, dd_s.at[p, xr], dd_r.at[p, xr], partner)

    def rpiece(s, xx):
        return rbuf.at[s, :, pl.ds(pl.multiple_of((y * 4 + xx) * 48, 16), 48), :]

    def rblock(s, yy, k0=0, nk=4):
        return rbuf.at[s, pl.ds(k0, nk), pl.ds(pl.multiple_of(yy * 192, 16), 192), :]

    def ra_copy(s, d):
        return remote(rs.at[(x + d) % 4, s], rpiece(s, x), ra_s.at[s, d - 1], ra_r.at[s, 4 - d], at_x(d))

    def ra_local(s):
        return pltpu.make_async_copy(rs.at[x, s], rpiece(s, x), ra_r.at[s, 0])

    def rd_copy(s, way):
        ref = rblock(s, y)
        return remote(ref, ref, rd_s.at[s, way], rd_r.at[s, way], at_y(1 if way == 0 else 3))

    def rr_copy(s, way):
        ref = rblock(s, (y + (3 if way == 0 else 1)) % 4, 2 * way, 2)
        return remote(ref, ref, rr_s.at[s, way], rr_r.at[s, way], at_y(1 if way == 0 else 3))

    def h_copy(xr, s, way):
        return remote(
            hs.at[xr, s, way], hr.at[xr, s, way], h_s.at[xr, s, way], h_r.at[xr, s, way], at_z(1 if way == 0 else 3)
        )

    def z_copy(way, xr, s):
        return remote(
            zs.at[way, xr, s], zr.at[way, xr, s], z_s.at[way, xr, s], z_r.at[way, xr, s], at_z(1 + 2 * way)
        )

    def x0_copy(s, d):
        return remote(xs0.at[s, d - 1], xr0.at[s, d - 1], x0_s.at[s, d - 1], x0_r.at[s, d - 1], at_x(d))

    def x1_copy(s, d):
        return remote(xs1.at[s, d - 1], xr1.at[s, d - 1], x1_s.at[s, d - 1], x1_r.at[s, d - 1], at_x(d))

    def ra_start(s):
        for d in (1, 3, 2):
            ra_copy(s, d).start()

    def ra_wait(s):
        for d in range(4):
            arrived(rpiece(s, (x + d) % 4), ra_r.at[s, d])

    def rd_start(s):
        for way in (0, 1):
            rd_copy(s, way).start()

    def rd_wait(s):
        for way in (0, 1):
            arrived(rblock(s, (y + (3 if way == 0 else 1)) % 4), rd_r.at[s, way])

    def rr_start(s):
        for way in (0, 1):
            rr_copy(s, way).start()

    def rr_wait(s):
        for way in (0, 1):
            arrived(rblock(s, (y + 2) % 4, 2 * way, 2), rr_r.at[s, way])

    def la_wait(p):
        d = rel_of(p)
        arrived(lpiece(y_at(p), x), la_r.at[d])
        dd_copy(p, 0).start()

    def ld_start(p):
        for way in (0, 1):
            ld_copy(p, way).start()

    def ld_wait(p):
        for way in (0, 1):
            xr = 3 if way == 0 else 1
            arrived(lpiece(y_at(p), (x + xr) % 4), ld_r.at[p, way])
            dd_copy(p, xr).start()

    def lr_start(p):
        for way in (0, 1):
            lr_copy(p, way).start()

    def lr_done(p):
        for way in (0, 1):
            arrived(lpiece(y_at(p), (x + 2) % 4, 48 * way, 48), lr_r.at[p, way])
        dd_copy(p, 2).start()

    def dd_wait(p, xr):
        arrived(lpiece(y_at(p), (x + xr) % 4, side=1 - core), dd_r.at[p, xr])

    def product(p, pieces, s):
        left = jnp.concatenate(
            [
                jnp.concatenate([lbuf[y_at(p) * 4 + (x + xr) % 4, k] for k in range(4)], axis=1)
                for xr in pieces
            ],
            axis=0,
        )
        return jnp.dot(left, rbuf[s].reshape(3072, NB), preferred_element_type=jnp.float32)

    def give_on(value, off, xr, s):
        @pl.when(off == 0)
        def _():
            own[s, xr] = value

        @pl.when(off == 2)
        def _():
            for way in (0, 1):
                write_coded(hs.at[xr, s, way], value[HROWS * way : HROWS * (way + 1)])
                h_copy(xr, s, way).start()

        for way in (0, 1):

            @pl.when(off == 1 + 2 * way)
            def _(way=way):
                arrived(hr.at[xr, s, way], h_r.at[xr, s, way])
                more = restored(hr.at[xr, s, way], HROWS)
                first, second = value[0:HROWS], value[HROWS:QROWS]
                if way == 0:
                    first = first + more
                else:
                    second = second + more
                write_coded(zs.at[way, xr, s], jnp.concatenate([first, second], axis=0))
                z_copy(way, xr, s).start()

    barrier = pltpu.get_barrier_semaphore()
    for device in everyone:
        pl.semaphore_signal(barrier, inc=1, device_id=device, device_id_type=MESH)
    pl.semaphore_wait(barrier, len(everyone))

    la_local().start()
    for s in range(NS):
        ra_local(s).start()

    does = {
        "ra": ra_start, "rd": rd_start, "rr": rr_start, "ld": ld_start, "lr": lr_start,
        "la": lambda d: la_copy(d).start(),
        "RA": ra_wait, "RD": rd_wait, "RR": rr_wait, "LA": la_wait, "LD": ld_wait, "LR": lr_done,
        "DD": lambda k: [dd_wait(k[0], xr) for xr in ((0,), (1, 3), (2,))[k[1]]],
    }

    def look(i):
        codes = [p * 32 + kind * 8 + s for p, kind, s in BLOCKS]
        word = 0
        for n in range(0, len(codes), 4):
            word = jnp.where(i // 4 == n // 4, sum(c * 128**m for m, c in enumerate(codes[n : n + 4])), word)
        m = i % 4
        shift = jnp.where(m == 0, 1, jnp.where(m == 1, 128, jnp.where(m == 2, 128**2, 128**3)))
        code = word // shift % 128
        return (i >= 0) & (i < len(codes)), code // 32, code // 8 % 4, code % 8

    def reduce(s, part):
        pieces = PARTS[part]
        sent, begin = (xs0, x0_copy) if part == 0 else (xs1, x1_copy)
        for xr in pieces:
            total = own[s, xr]
            for way in (0, 1):
                arrived(zr.at[way, xr, s], z_r.at[way, xr, s])
                total = total + restored(zr.at[way, xr, s], QROWS)
            tot[xr] = total

        def rows_of(i):
            return [
                tot[xr, pl.ds(pl.multiple_of(side * 96 + i * 24, 8), 24), :] for xr in pieces for side in range(2)
            ]

        def give(d, carry):
            write_coded(sent.at[s, d - 1], jnp.concatenate(rows_of((x + d) % 4), axis=0))
            begin(s, d).start()
            return carry

        lax.fori_loop(1, 4, give, 0)
        own_rows = rows_of(x)
        for n, xr in enumerate(pieces):
            kept[s, xr] = jnp.concatenate(own_rows[2 * n : 2 * n + 2], axis=0)

    def round_(i, carry):
        def events(n):
            todo = [(what, k) for m, what, k in EVENTS if m == n]
            if todo:

                @pl.when(i == n)
                def _():
                    for what, k in todo:
                        does[what](k)

        for g in range(0, len(BLOCKS), 9):
            if any(g <= m < g + 9 for m, _, _ in EVENTS):

                @pl.when((i >= g) & (i < g + 9))
                def _(g=g):
                    for n in range(g, g + 9):
                        events(n)

        def half(j, carry):
            there, p, kind, s = look(i - LAG * j)
            off = (y_at(p) - z + 4) % 4

            @pl.when(there & (off % 2 == j))
            def _():
                @pl.when(kind == 1)
                def _():
                    val[...] = product(p, (1, 3), s).reshape(2, QROWS, NB)

                @pl.when(kind != 1)
                def _():
                    val[0] = product(p, (kind,), s)

                def one(n, carry):
                    give_on(val[n], off, jnp.where(kind == 1, 1 + 2 * n, kind), s)
                    return carry

                lax.fori_loop(0, jnp.where(kind == 1, 2, 1), one, 0)

            return carry

        lax.fori_loop(0, 2, half, 0)

        for part in range(2):

            def sums(s, carry, part=part):
                reduce(s, part)
                return carry

            begun = sum(jnp.where(i > n, 1, 0) for n in SUMS[part])
            lax.fori_loop(begun, sum(jnp.where(i >= n, 1, 0) for n in SUMS[part]), sums, 0)
        return carry

    lax.fori_loop(0, ROUNDS, round_, 0)

    for d in (1, 2, 3):
        la_copy(d).wait_send()

    def sent_right(s, carry):
        for d in (1, 2, 3):
            ra_copy(s, d).wait_send()
        for way in (0, 1):
            rd_copy(s, way).wait_send()
            rr_copy(s, way).wait_send()
        return carry

    def sent_left(q, carry):
        for way in (0, 1):
            ld_copy(q, way).wait_send()
            lr_copy(q, way).wait_send()
        for xr in range(4):
            dd_copy(q, xr).wait_send()
        return carry

    def sent_z(n, carry):
        for way in (0, 1):
            h_copy(n // 6, n % 6, way).wait_send()
            z_copy(way, n // 6, n % 6).wait_send()
        return carry

    lax.fori_loop(0, NS, sent_right, 0)
    lax.fori_loop(0, 4, sent_left, 0)
    lax.fori_loop(0, 24, sent_z, 0)

    def finish(s, carry):
        for d in (1, 2, 3):
            arrived(xr0.at[s, d - 1], x0_r.at[s, d - 1])
            arrived(xr1.at[s, d - 1], x1_r.at[s, d - 1])
            x0_copy(s, d).wait_send()
            x1_copy(s, d).wait_send()
        return carry

    lax.fori_loop(0, NS, finish, 0)


def place_kernel(kept, came0, came1, out):
    x = lax.axis_index("row") % 4
    for bt in range(3):
        for d in range(4):
            source = (x - d + 4) % 4
            if d:
                first, last = restored(came0.at[bt, d - 1], 144), restored(came1.at[bt, d - 1], 48)
            for n, xr in enumerate((0, 1, 3, 2)):
                value = kept[bt, xr] if d == 0 else last if xr == 2 else first[48 * n : 48 * n + 48]
                at = pl.multiple_of((source + xr) % 4 * 48, 8)
                out[0, source, 0, pl.ds(at, 48), bt * NB : bt * NB + NB] = value


def right_kernel(mask, w, rs):
    first = lax.axis_index("row") * 48
    tile = first // TILE
    after = jnp.minimum(tile + 1, 5)
    edge = (tile + 1) * TILE - first
    upper = lax.broadcasted_iota(jnp.int32, (48, TILE), 0) < edge
    rows = jnp.swapaxes(w[0], 0, 1)
    low, high = mask[0, tile].astype(jnp.float32), mask[0, after].astype(jnp.float32)
    for j in range(8):
        for b in range(6):
            kept = jnp.where(upper, low[j : j + 1, b : b + 1], high[j : j + 1, b : b + 1])
            rs[j // 2, j % 2 * 3 + b // 2, 0, :, b % 2 * TILE : (b % 2 + 1) * TILE] = (
                rows[j, :, b * TILE : (b + 1) * TILE] * kept.astype(jnp.bfloat16)
            )


def on_device(amplitudes, integrals, pair_mask, tile_mask):
    kept = jnp.where(pair_mask[:, :, None, None] != 0, amplitudes, jnp.zeros((), jnp.bfloat16))
    ls = kept.reshape(4, 4, 4, 24, 768).transpose(0, 2, 1, 3, 4).reshape(4, 4, 96, 768)
    rs = pl.pallas_call(
        right_kernel,
        grid=(4,),
        out_shape=jax.ShapeDtypeStruct((4, NS, 4, 48, NB), jnp.bfloat16),
        in_specs=[
            pl.BlockSpec((1, 6, 8, 6), lambda k: (k, 0, 0, 0)),
            pl.BlockSpec((1, 48, 8, 768), lambda k: (k, 0, 0, 0)),
        ],
        out_specs=pl.BlockSpec((4, NS, 1, 48, NB), lambda k: (0, 0, k, 0, 0)),
        cost_estimate=pl.CostEstimate(flops=10**6, bytes_accessed=5 * 10**6, transcendentals=0),
    )(tile_mask, integrals)
    dma = pltpu.SemaphoreType.DMA
    bf, i16, f32 = jnp.bfloat16, jnp.int16, jnp.float32
    came = ((NS, 3) + coded_shape(144), (NS, 3) + coded_shape(48))
    parts = pl.pallas_call(
        kernel,
        out_shape=(
            jax.ShapeDtypeStruct((NS, 4, 48, NB), f32),
            jax.ShapeDtypeStruct(came[0], i16),
            jax.ShapeDtypeStruct(came[1], i16),
        ),
        in_specs=[pl.BlockSpec(memory_space=pl.ANY)] * 2,
        out_specs=[pl.BlockSpec(memory_space=pltpu.VMEM)] * 3,
        scratch_shapes=[
            pltpu.VMEM((16, 4, 192, 768), bf),
            pltpu.VMEM((NS, 4, 768, NB), bf),
            pltpu.VMEM((NS, 4, QROWS, NB), f32),
            pltpu.VMEM((4, QROWS, NB), f32),
            pltpu.VMEM((2, QROWS, NB), f32),
            pltpu.VMEM((4, NS, 2) + coded_shape(HROWS), i16),
            pltpu.VMEM((4, NS, 2) + coded_shape(HROWS), i16),
            pltpu.VMEM((2, 4, NS) + coded_shape(QROWS), i16),
            pltpu.VMEM((2, 4, NS) + coded_shape(QROWS), i16),
            pltpu.VMEM((NS, 3) + coded_shape(144), i16),
            pltpu.VMEM((NS, 3) + coded_shape(48), i16),
            dma((3,)), dma((4,)), dma((4, 2)), dma((4, 2)), dma((4, 2)), dma((4, 2)), dma((4, 4)), dma((4, 4)),
            dma((NS, 3)), dma((NS, 4)), dma((NS, 2)), dma((NS, 2)), dma((NS, 2)), dma((NS, 2)),
            dma((4, NS, 2)), dma((4, NS, 2)), dma((2, 4, NS)), dma((2, 4, NS)), dma((NS, 3)), dma((NS, 3)),
            dma((NS, 3)), dma((NS, 3)),
        ],
        compiler_params=pltpu.CompilerParams(
            collective_id=0, has_side_effects=True, vmem_limit_bytes=63 * 2**20
        ),
        cost_estimate=pl.CostEstimate(flops=29 * 10**9, bytes_accessed=10**7, transcendentals=0),
    )(ls, rs)
    done = pl.pallas_call(
        place_kernel,
        grid=(2,),
        out_shape=jax.ShapeDtypeStruct((1, 4, 2, QROWS, 768), f32),
        in_specs=[
            pl.BlockSpec((3, 4, 48, NB), lambda s: (s, 0, 0, 0)),
            pl.BlockSpec((3,) + came[0][1:], lambda s: (s, 0, 0, 0)),
            pl.BlockSpec((3,) + came[1][1:], lambda s: (s, 0, 0, 0)),
        ],
        out_specs=pl.BlockSpec((1, 4, 1, QROWS, 768), lambda s: (0, 0, s, 0, 0)),
        cost_estimate=pl.CostEstimate(flops=10**7, bytes_accessed=8 * 10**6, transcendentals=0),
    )(*parts)
    return done.reshape(1, 8, QROWS, 768)


def solution(mesh):
    placed = (
        P(None, "rep", ("row", "col"), None),
        P("rep", "row", "col", None),
        P(None, "rep"),
        P("rep", None, "col", None),
    )
    return jax.shard_map(
        on_device,
        mesh=mesh,
        in_specs=placed,
        out_specs=P("row", "col", "rep", None),
        check_vma=False,
    )
```
